512 devices in a mesh: blk: 32 (over x, z_hi, core), col: 16 (over y, z_lo).
Axes of the slice: x: 4, y: 8, z: 8 (z_hi: 4, z_lo: 2; z = z_hi * 2 + z_lo), core: 2. Of those that a mesh axis runs over, the one named last changes fastest.
Arguments:
- features: float32 [8, 65536], P(None, ('blk', 'col')), may hold values from -6 to 6
- vectors: float32 [16, 65536], P(None, ('blk', 'col')), may hold values from -0.0234375 to 0.0234375
- lengthscales: float32 [8], replicated, may hold values from 0.7 to 3
- noise_var: float32 [65536], P(('blk', 'col')), may hold values from 0.5 to 64
- signal: float32 [1], replicated, may hold values from 0.5 to 2
Outputs:
- product: float32 [16, 65536], P(None, ('blk', 'col'))
The draws below stay inside these ranges and needn't reach their ends.
All inputs are finite; a program needn't handle non-finite values.
Results may differ from the reference program's by a relative error of at most 0.00005.
Values sent between devices are 32-bit elements; how exact they have to be, the bound alone decides.
A program may use at most 64 MiB of HBM per device.

```python
import math
import jax
import jax.numpy as jnp
from jax import lax

FEAT = 8
PROBES = 16
PTS_DEV = 128
POINTS = 65536


def block_levels(key, shape, cuts, least, largest):
    level = 1.0
    for dim, shards_of in cuts:
        steps = jax.random.uniform(jax.random.fold_in(jax.random.fold_in(key, 6), dim), (shards_of,), jnp.float32, least / len(cuts), largest / len(cuts))
        level = level * jnp.repeat(jnp.exp(steps), shape[dim] // shards_of).reshape((-1,) + (1,) * (len(shape) - 1 - dim))
    return level


def bell_draw(key, dims, scale, most, shards=(), held_as=jnp.bfloat16):
    array = scale * jax.random.normal(key, dims, jnp.float32)
    if shards:
        array = array * block_levels(key, dims, shards, -0.22, 0.18)
    return jnp.clip(array, -most, most).astype(held_as)


def setup_inputs(seed: int = 0) -> dict:
    arg_keys = jax.random.split(jax.random.key(seed), 6)
    return {
        "features": bell_draw(arg_keys[0], (FEAT, POINTS), 1.0, 6.0, ((1, 512),), jnp.float32),
        "vectors": bell_draw(arg_keys[1], (PROBES, POINTS), POINTS ** -0.5, 0.0234375, ((1, 512),), jnp.float32),
        "lengthscales": jnp.clip(jnp.exp(jax.random.uniform(arg_keys[2], (FEAT,), jnp.float32, math.log(0.7), math.log(3.0))), 0.7, 3.0),
        "noise_var": jnp.clip(jnp.exp(math.log(64.0) - 4.8520303 * jax.random.uniform(arg_keys[3], (POINTS,), jnp.float32) ** block_levels(arg_keys[3], (POINTS,), ((0, 512),), -0.2, 0.2)), 0.5, 64.0),
        "signal": jnp.clip(jnp.exp(jax.random.uniform(arg_keys[4], (1,), jnp.float32, math.log(0.5), math.log(2.0))), 0.5, 2.0),
    }


ROOT_FIVE = 2.23606797749979

def matern_tile(rows_x, rows_sq, cols_x, cols_sq):
    cross = lax.dot_general(rows_x, cols_x, (((0,), (0,)), ((), ())), precision=lax.Precision.HIGHEST, preferred_element_type=jnp.float32)
    dist_sq = jnp.maximum(rows_sq[:, None] + cols_sq[None, :] - 2.0 * cross, 0.0)
    scaled_dist = ROOT_FIVE * jnp.sqrt(dist_sq)
    return (1.0 + scaled_dist + scaled_dist * scaled_dist / 3.0) * jnp.exp(-scaled_dist)

def reference(features, vectors, lengthscales, noise_var, signal):
    scaled = features / lengthscales[:, None]
    sq_norm = lax.optimization_barrier(jnp.sum(scaled * scaled, axis=0))
    count = POINTS // PTS_DEV
    row_blocks = scaled.reshape(FEAT, count, PTS_DEV).transpose(1, 0, 2)
    sq_blocks = sq_norm.reshape(count, PTS_DEV)

    def one_block(pair):
        block_x, block_sq = pair
        kernel_tile = matern_tile(block_x, block_sq, scaled, sq_norm)
        return lax.dot_general(vectors, kernel_tile, (((1,), (1,)), ((), ())), precision=lax.Precision.HIGHEST, preferred_element_type=jnp.float32)
    sums = lax.map(one_block, (row_blocks, sq_blocks))
    sums = sums.transpose(1, 0, 2).reshape(PROBES, POINTS)
    return signal[0] * sums + noise_var[None, :] * vectors
```

```python
import functools
import math

import jax
import jax.numpy as jnp
from jax import lax
from jax.experimental import pallas as pl
from jax.experimental.pallas import tpu as pltpu
from jax.sharding import PartitionSpec as P

MESH = pl.DeviceIdType.MESH
F32 = jnp.float32
BF16 = jnp.bfloat16
SCALE = math.sqrt(5.0 / 3.0)
HALF3 = math.sqrt(3.0) / 2.0
RATE = -math.sqrt(3.0) * math.log2(math.e)
TINY = 1e-30
WIDTH = 128
FEAT = 8
PROBES = 16
DEPTH = 64


def split3(value):
    high = value.astype(BF16).astype(F32)
    rest = value - high
    mid = rest.astype(BF16).astype(F32)
    return high, mid, rest - mid


def norms3(points):
    return split3(jnp.sum(points * points, axis=0, keepdims=True))


def row_side(points):
    high, mid, low = split3(points)
    nh, nm, nl = norms3(points)
    one, zero = jnp.ones_like(nh), jnp.zeros_like(nh)
    extra = jnp.concatenate([nh, nm, nl, one, one, one, zero, zero], axis=0)
    pad = jnp.zeros_like(points)
    return jnp.concatenate([high, high, mid, mid, high, low, extra, pad], axis=0)


def col_side(points):
    high, mid, low = (-2.0 * part for part in split3(points))
    nh, nm, nl = norms3(points)
    one, zero = jnp.ones_like(nh), jnp.zeros_like(nh)
    extra = jnp.concatenate([one, one, one, nh, nm, nl, zero, zero], axis=0)
    pad = jnp.zeros_like(points)
    return jnp.concatenate([high, mid, high, mid, low, high, extra, pad], axis=0)


def matern(dist_sq):
    floor = jnp.maximum(dist_sq, TINY)
    dist = floor * lax.rsqrt(floor)
    decay = jnp.exp2(dist * RATE)
    shifted = dist + HALF3
    return (shifted * shifted + 0.25) * decay


def tile_sums(cols_t, vecs, rows):
    kernel_tile = matern(jnp.dot(cols_t, rows, preferred_element_type=F32))
    high = kernel_tile.astype(BF16)
    low = (kernel_tile - high.astype(F32)).astype(BF16)
    both = jnp.dot(vecs, high, preferred_element_type=F32)
    return both[:PROBES] + both[PROBES:] + jnp.dot(vecs[:PROBES], low, preferred_element_type=F32)


def kernel(nb, nc, ls_ref, feat_ref, vec_ref, out_ref, mine, colbuf, rowbuf, rows, cols_t, vecs, acc, parts,
           row_send, row_recv, col_send, col_recv, part_send, part_recv):
    blk, col = lax.axis_index("blk"), lax.axis_index("col")

    def row_peer(step):
        return (blk, lax.rem(col + step, nc))

    def col_peer(step):
        return (lax.rem(blk + step, nb), col)

    barrier = pltpu.get_barrier_semaphore()

    def greet(peer):
        def body(step, carry):
            pl.semaphore_signal(barrier, inc=1, device_id=peer(step), device_id_type=MESH)
            return carry
        return body

    lax.fori_loop(1, nc, greet(row_peer), 0)
    lax.fori_loop(1, nb, greet(col_peer), 0)

    feature = lax.broadcasted_iota(jnp.int32, (FEAT, WIDTH), 0)
    lengths = jnp.full((FEAT, WIDTH), ls_ref[0], F32)
    for k in range(1, FEAT):
        lengths = jnp.where(feature == k, ls_ref[k], lengths)
    mine[:FEAT] = feat_ref[...] / lengths * SCALE
    mine[FEAT:] = vec_ref[...]
    acc[...] = jnp.zeros_like(acc)
    pl.semaphore_wait(barrier, nb + nc - 2)

    def row_copy(step):
        return pltpu.make_async_remote_copy(
            src_ref=mine.at[:FEAT], dst_ref=rowbuf.at[step], send_sem=row_send.at[step], recv_sem=row_recv.at[step],
            device_id=row_peer(step), device_id_type=MESH)

    def col_copy(step):
        return pltpu.make_async_remote_copy(
            src_ref=mine, dst_ref=colbuf.at[step], send_sem=col_send.at[step], recv_sem=col_recv.at[step],
            device_id=col_peer(step), device_id_type=MESH)

    def part_copy(step):
        return pltpu.make_async_remote_copy(
            src_ref=acc.at[step], dst_ref=parts.at[step], send_sem=part_send.at[step], recv_sem=part_recv.at[step],
            device_id=(blk, lax.rem(col + nc - step, nc)), device_id_type=MESH)

    def run(action):
        def body(step, carry):
            action(step)
            return carry
        return body

    lax.fori_loop(1, nc, run(lambda step: row_copy(step).start()), 0)
    lax.fori_loop(1, nb, run(lambda step: col_copy(step).start()), 0)

    def put_row(step, points):
        rows[:DEPTH, pl.ds(pl.multiple_of(step * WIDTH, WIDTH), WIDTH)] = row_side(points).astype(BF16)

    def put_col(step, block):
        at = pl.ds(pl.multiple_of(step * WIDTH, WIDTH), WIDTH)
        tall = jnp.concatenate([col_side(block[:FEAT]), jnp.zeros((WIDTH - DEPTH, WIDTH), F32)], axis=0)
        cols_t[at, :] = tall.T.astype(BF16)
        high = block[FEAT:].astype(BF16)
        vecs[:PROBES, at] = high
        vecs[PROBES:, at] = (block[FEAT:] - high.astype(F32)).astype(BF16)

    rows[DEPTH:, :] = jnp.zeros((WIDTH - DEPTH, nc * WIDTH), BF16)
    put_row(0, mine[:FEAT])
    put_col(0, mine[...])

    def arrived_row(step, carry):
        row_copy(step).wait_recv()
        put_row(step, rowbuf[step])
        return carry

    lax.fori_loop(1, nc, arrived_row, 0)

    def arrived_col(step):
        col_copy(step).wait_recv()
        put_col(step, colbuf[step])

    def sums(first_col, col_count, first_row, row_count):
        at = pl.ds(pl.multiple_of(first_col * WIDTH, WIDTH), col_count * WIDTH)
        rows_at = pl.ds(pl.multiple_of(first_row * WIDTH, WIDTH), row_count * WIDTH)
        return tile_sums(cols_t[at, :], vecs[:, at], rows[:, rows_at])

    half = nb // 2

    def strip(pair, carry):
        @pl.when(pair > 0)
        def _():
            arrived_col(2 * pair)
        arrived_col(2 * pair + 1)
        total = sums(2 * pair, 2, 0, nc)
        for k in range(nc):
            acc[k] += total[:, k * WIDTH:(k + 1) * WIDTH]
        return carry

    lax.fori_loop(0, half // 2, strip, 0)
    lax.fori_loop(half, nb, run(arrived_col), 0)

    def chunk(turn, carry):
        first = nc - 2 - 2 * turn
        total = sums(half, nb - half, first, 2)
        for k in range(2):
            acc[first + k] += total[:, k * WIDTH:(k + 1) * WIDTH]
        part_copy(first + 1).start()

        @pl.when(first > 0)
        def _():
            part_copy(first).start()
        return carry

    lax.fori_loop(0, nc // 2, chunk, 0)
    lax.fori_loop(1, nc, run(lambda step: row_copy(step).wait_send()), 0)
    lax.fori_loop(1, nb, run(lambda step: col_copy(step).wait_send()), 0)
    lax.fori_loop(1, nc, run(lambda step: part_copy(step).wait_send()), 0)

    def add_part(step, total):
        part_copy(step).wait_recv()
        return total + parts[step]

    out_ref[...] = lax.fori_loop(1, nc, add_part, acc[0])


def on_device(nb, nc, features, vectors, lengthscales, noise_var, signal):
    sums = pl.pallas_call(
        functools.partial(kernel, nb, nc),
        out_shape=jax.ShapeDtypeStruct((PROBES, WIDTH), F32),
        in_specs=[
            pl.BlockSpec(memory_space=pltpu.SMEM),
            pl.BlockSpec(memory_space=pltpu.VMEM),
            pl.BlockSpec(memory_space=pltpu.VMEM),
        ],
        out_specs=pl.BlockSpec(memory_space=pltpu.VMEM),
        scratch_shapes=[
            pltpu.VMEM((FEAT + PROBES, WIDTH), F32),
            pltpu.VMEM((nb, FEAT + PROBES, WIDTH), F32),
            pltpu.VMEM((nc, FEAT, WIDTH), F32),
            pltpu.VMEM((WIDTH, nc * WIDTH), BF16),
            pltpu.VMEM((nb * WIDTH, WIDTH), BF16),
            pltpu.VMEM((2 * PROBES, nb * WIDTH), BF16),
            pltpu.VMEM((nc, PROBES, WIDTH), F32),
            pltpu.VMEM((nc, PROBES, WIDTH), F32),
            pltpu.SemaphoreType.DMA((nc,)),
            pltpu.SemaphoreType.DMA((nc,)),
            pltpu.SemaphoreType.DMA((nb,)),
            pltpu.SemaphoreType.DMA((nb,)),
            pltpu.SemaphoreType.DMA((nc,)),
            pltpu.SemaphoreType.DMA((nc,)),
        ],
        compiler_params=pltpu.CompilerParams(
            collective_id=0, has_side_effects=True, vmem_limit_bytes=48 * 1024 * 1024
        ),
        name="matern_sums",
    )(lengthscales, features, vectors)
    return signal[0] * sums + noise_var[None, :] * vectors


def solution(mesh):
    nb, nc = mesh.shape["blk"], mesh.shape["col"]
    placed = (P(None, ("blk", "col")), P(None, ("blk", "col")), P(), P(("blk", "col")), P())
    return jax.shard_map(
        functools.partial(on_device, nb, nc),
        mesh=mesh,
        in_specs=placed,
        out_specs=P(None, ("blk", "col")),
        check_vma=False,
    )
```

```python
import functools
import math

import jax
import jax.numpy as jnp
from jax import lax
from jax.experimental import pallas as pl
from jax.experimental.pallas import tpu as pltpu
from jax.sharding import PartitionSpec as P

MESH = pl.DeviceIdType.MESH
F32 = jnp.float32
BF16 = jnp.bfloat16
SCALE = math.sqrt(5.0 / 3.0)
HALF3 = math.sqrt(3.0) / 2.0
RATE = -math.sqrt(3.0) * math.log2(math.e)
TINY = 1e-30
WIDTH = 128
FEAT = 8
PROBES = 16
DEPTH = 64


def split3(value):
    high = value.astype(BF16).astype(F32)
    rest = value - high
    mid = rest.astype(BF16).astype(F32)
    return high, mid, rest - mid


def norms3(points):
    return split3(jnp.sum(points * points, axis=0, keepdims=True))


def row_side(points):
    high, mid, low = split3(points)
    nh, nm, nl = norms3(points)
    one, zero = jnp.ones_like(nh), jnp.zeros_like(nh)
    extra = jnp.concatenate([nh, nm, nl, one, one, one, zero, zero], axis=0)
    pad = jnp.zeros_like(points)
    return jnp.concatenate([high, high, mid, mid, high, low, extra, pad], axis=0)


def col_side(points):
    high, mid, low = (-2.0 * part for part in split3(points))
    nh, nm, nl = norms3(points)
    one, zero = jnp.ones_like(nh), jnp.zeros_like(nh)
    extra = jnp.concatenate([one, one, one, nh, nm, nl, zero, zero], axis=0)
    pad = jnp.zeros_like(points)
    return jnp.concatenate([high, mid, high, mid, low, high, extra, pad], axis=0)


def matern(dist_sq):
    floor = jnp.maximum(dist_sq, TINY)
    dist = floor * lax.rsqrt(floor)
    decay = jnp.exp2(dist * RATE)
    shifted = dist + HALF3
    return (shifted * shifted + 0.25) * decay


def halves(value):
    high = value.astype(BF16)
    return high, (value - high.astype(F32)).astype(BF16)


def fold(both):
    return both[:PROBES] + both[PROBES:]


def times(vecs, high, low, dims):
    first = lax.dot_general(vecs, high, dims, preferred_element_type=F32)
    return fold(first) + lax.dot_general(vecs[:PROBES], low, dims, preferred_element_type=F32)


OVER_ROWS = (((1,), (0,)), ((), ()))
OVER_COLS = (((1,), (1,)), ((), ()))


def kernel(nb, nc, ls_ref, feat_ref, vec_ref, out_ref, rowbuf, colbuf, rows_t, row_vecs, cols, col_vecs,
           row_acc, col_acc, row_parts, col_parts, dist0, dist1, high0, high1, low0, low1,
           row_send, row_recv, col_send, col_recv, rp_send, rp_recv, cp_send, cp_recv):
    blk, col = lax.axis_index("blk"), lax.axis_index("col")
    half = nb // 2
    pairs, chunks = half // 2, nc // 2
    dist, highs, lows = (dist0, dist1), (high0, high1), (low0, low1)
    mine = rowbuf.at[0]

    def loop(first, last, action):
        def body(step, carry):
            action(step)
            return carry
        lax.fori_loop(first, last, body, 0)

    def row_peer(step):
        return (blk, lax.rem(col + step, nc))

    def row_owner(step):
        return (blk, lax.rem(col + nc - step, nc))

    def col_peer(step):
        return (lax.rem(blk + step, nb), col)

    def col_owner(step):
        return (lax.rem(blk + nb - step, nb), col)

    barrier = pltpu.get_barrier_semaphore()

    def greet(peer):
        return lambda step: pl.semaphore_signal(barrier, inc=1, device_id=peer(step), device_id_type=MESH)

    loop(1, nc, greet(row_owner))
    loop(1, half + 1, greet(col_owner))

    feature = lax.broadcasted_iota(jnp.int32, (FEAT, WIDTH), 0)
    lengths = jnp.full((FEAT, WIDTH), ls_ref[0], F32)
    for k in range(1, FEAT):
        lengths = jnp.where(feature == k, ls_ref[k], lengths)
    scaled = feat_ref[...] / lengths * SCALE
    rowbuf[0, :FEAT] = scaled
    rowbuf[0, FEAT:] = vec_ref[...]
    colbuf[half - 1, :FEAT] = scaled
    colbuf[half - 1, FEAT:] = vec_ref[...]
    colbuf[half + 1] = jnp.zeros((FEAT + PROBES, WIDTH), F32)
    row_acc[...] = jnp.zeros_like(row_acc)
    col_acc[...] = jnp.zeros_like(col_acc)
    high1[...] = jnp.zeros_like(high1)
    low1[...] = jnp.zeros_like(low1)
    cols[DEPTH:, :] = jnp.zeros((WIDTH - DEPTH, cols.shape[1]), BF16)
    pl.semaphore_wait(barrier, nc - 1 + half)

    def row_copy(step):
        return pltpu.make_async_remote_copy(
            src_ref=mine, dst_ref=rowbuf.at[step], send_sem=row_send.at[step], recv_sem=row_recv.at[step],
            device_id=row_peer(step), device_id_type=MESH)

    def col_copy(place):
        return pltpu.make_async_remote_copy(
            src_ref=mine, dst_ref=colbuf.at[place], send_sem=col_send.at[place], recv_sem=col_recv.at[place],
            device_id=col_peer(jnp.where(place == half, half, place + 1)), device_id_type=MESH)

    def row_part(step):
        return pltpu.make_async_remote_copy(
            src_ref=row_acc.at[step], dst_ref=row_parts.at[step], send_sem=rp_send.at[step], recv_sem=rp_recv.at[step],
            device_id=row_owner(step), device_id_type=MESH)

    def col_part(place):
        return pltpu.make_async_remote_copy(
            src_ref=col_acc.at[place], dst_ref=col_parts.at[place], send_sem=cp_send.at[place],
            recv_sem=cp_recv.at[place], device_id=col_owner(place + 1), device_id_type=MESH)

    loop(1, nc, lambda step: row_copy(step).start())
    loop(0, half - 1, lambda place: col_copy(place).start())
    col_copy(half).start()

    def span(place, count):
        return pl.ds(pl.multiple_of(place * WIDTH, WIDTH), count * WIDTH)

    def put_cols(pair):
        for k in range(2):
            block = colbuf[2 * pair + k]
            at = span(2 * pair + k, 1)
            cols[:DEPTH, at] = col_side(block[:FEAT]).astype(BF16)
            share = jnp.where(2 * pair + k == half - 1, 0.5, 1.0)
            high, low = halves(block[FEAT:] * share)
            col_vecs[:PROBES, at] = high
            col_vecs[PROBES:, at] = low

    def inner(place, count, chunk, into):
        at = pl.ds(chunk * 2 * WIDTH, 2 * WIDTH)
        into[:, :count * WIDTH] = jnp.dot(rows_t[at, :], cols[:, span(place, count)], preferred_element_type=F32)

    def elementwise(which, count):
        at = slice(0, count * WIDTH)
        high, low = halves(matern(dist[which][:, at]))
        highs[which][:, at] = high
        lows[which][:, at] = low

    def add_rows(place, count, chunk, which):
        at = slice(0, count * WIDTH)
        total = times(col_vecs[:, span(place, count)], highs[which][:, at], lows[which][:, at], OVER_COLS)
        for k in range(2):
            row_acc[2 * chunk + k] += total[:, k * WIDTH:(k + 1) * WIDTH]

    def add_cols(place, chunk, which):
        total = times(row_vecs[:, chunk * 2 * WIDTH:(chunk + 1) * 2 * WIDTH], highs[which][...], lows[which][...], OVER_ROWS)
        for k in range(2):
            col_acc[place + k] += total[:, k * WIDTH:(k + 1) * WIDTH]

    loop(1, nc, lambda step: row_copy(step).wait_recv())
    for step in range(nc):
        at = slice(step * WIDTH, (step + 1) * WIDTH)
        tall = jnp.concatenate([row_side(rowbuf[step, :FEAT]), jnp.zeros((WIDTH - DEPTH, WIDTH), F32)], axis=0)
        rows_t[at, :] = tall.T.astype(BF16)
        high, low = halves(rowbuf[step, FEAT:])
        row_vecs[:PROBES, at] = high
        row_vecs[PROBES:, at] = low
    col_copy(0).wait_recv()
    col_copy(1).wait_recv()
    put_cols(0)
    inner(0, 2, 0, dist[0])

    def one_pair(pair):
        col_copy(2 * pair + 2).wait_recv()

        @pl.when(pair < pairs - 2)
        def _():
            col_copy(2 * pair + 3).wait_recv()
        put_cols(pair + 1)
        for chunk in range(chunks):
            now, other = chunk % 2, (chunk + 1) % 2
            if chunk + 1 < chunks:
                inner(2 * pair, 2, chunk + 1, dist[other])
            else:
                inner(2 * pair + 2, 2, 0, dist[other])
            elementwise(now, 2)
            before = 2 * pair if chunk > 0 else 2 * jnp.maximum(pair - 1, 0)
            add_cols(before, (chunk - 1) % chunks, other)
            add_rows(before, 2, (chunk - 1) % chunks, other)

        @pl.when(pair > 0)
        def _():
            col_part(2 * pair - 2).start()
            col_part(2 * pair - 1).start()

    loop(0, pairs, one_pair)
    for chunk in range(chunks + 1):
        now, other = chunk % 2, (chunk + 1) % 2
        if chunk + 1 < chunks:
            inner(half, 1, chunk + 1, dist[other])
        if chunk < chunks:
            elementwise(now, 1)
        if chunk == 0:
            add_cols(half - 2, chunks - 1, other)
            add_rows(half - 2, 2, chunks - 1, other)
            col_part(half - 2).start()
        else:
            add_rows(half, 1, chunk - 1, other)
            if chunk > 1:
                row_part(2 * chunk - 2).start()
            row_part(2 * chunk - 1).start()

    loop(1, nc, lambda step: row_copy(step).wait_send())
    loop(0, half - 1, lambda place: col_copy(place).wait_send())
    col_copy(half).wait_send()
    loop(0, half - 1, lambda place: col_part(place).wait_send())
    loop(1, nc, lambda step: row_part(step).wait_send())

    def add_col_part(place, total):
        col_part(place).wait_recv()
        return total + col_parts[place]

    def add_row_part(step, total):
        row_part(step).wait_recv()
        return total + row_parts[step]

    total = row_acc[0] + 0.5 * col_acc[half - 1]
    total = lax.fori_loop(0, half - 1, add_col_part, total)
    out_ref[...] = lax.fori_loop(1, nc, add_row_part, total)


def on_device(nb, nc, features, vectors, lengthscales, noise_var, signal):
    half = nb // 2
    sums = pl.pallas_call(
        functools.partial(kernel, nb, nc),
        out_shape=jax.ShapeDtypeStruct((PROBES, WIDTH), F32),
        in_specs=[
            pl.BlockSpec(memory_space=pltpu.SMEM),
            pl.BlockSpec(memory_space=pltpu.VMEM),
            pl.BlockSpec(memory_space=pltpu.VMEM),
        ],
        out_specs=pl.BlockSpec(memory_space=pltpu.VMEM),
        scratch_shapes=[
            pltpu.VMEM((nc, FEAT + PROBES, WIDTH), F32),
            pltpu.VMEM((half + 2, FEAT + PROBES, WIDTH), F32),
            pltpu.VMEM((nc * WIDTH, WIDTH), BF16),
            pltpu.VMEM((2 * PROBES, nc * WIDTH), BF16),
            pltpu.VMEM((WIDTH, (half + 2) * WIDTH), BF16),
            pltpu.VMEM((2 * PROBES, (half + 2) * WIDTH), BF16),
            pltpu.VMEM((nc, PROBES, WIDTH), F32),
            pltpu.VMEM((half, PROBES, WIDTH), F32),
            pltpu.VMEM((nc, PROBES, WIDTH), F32),
            pltpu.VMEM((half, PROBES, WIDTH), F32),
        ]
        + [pltpu.VMEM((2 * WIDTH, 2 * WIDTH), F32)] * 2
        + [pltpu.VMEM((2 * WIDTH, 2 * WIDTH), BF16)] * 4
        + [pltpu.SemaphoreType.DMA((count,)) for count in (nc, nc, half + 1, half + 1, nc, nc, half, half)],
        compiler_params=pltpu.CompilerParams(
            collective_id=0, has_side_effects=True, vmem_limit_bytes=48 * 1024 * 1024
        ),
        name="matern_sums",
    )(lengthscales, features, vectors)
    return signal[0] * sums + noise_var[None, :] * vectors


def solution(mesh):
    nb, nc = mesh.shape["blk"], mesh.shape["col"]
    placed = (P(None, ("blk", "col")), P(None, ("blk", "col")), P(), P(("blk", "col")), P())
    return jax.shard_map(
        functools.partial(on_device, nb, nc),
        mesh=mesh,
        in_specs=placed,
        out_specs=P(None, ("blk", "col")),
        check_vma=False,
    )
```

```python
import functools
import math

import jax
import jax.numpy as jnp
from jax import lax
from jax.experimental import pallas as pl
from jax.experimental.pallas import tpu as pltpu
from jax.sharding import PartitionSpec as P

MESH = pl.DeviceIdType.MESH
F32 = jnp.float32
BF16 = jnp.bfloat16
SCALE = math.sqrt(5.0 / 3.0)
HALF3 = math.sqrt(3.0) / 2.0
RATE = -math.sqrt(3.0) * math.log2(math.e)
TINY = 1e-30
WIDTH = 128
FEAT = 8
PROBES = 16
DEPTH = 64


def split3(value):
    high = value.astype(BF16).astype(F32)
    rest = value - high
    mid = rest.astype(BF16).astype(F32)
    return high, mid, rest - mid


def norms3(points):
    return split3(jnp.sum(points * points, axis=0, keepdims=True))


def row_side(points):
    high, mid, low = split3(points)
    nh, nm, nl = norms3(points)
    one, zero = jnp.ones_like(nh), jnp.zeros_like(nh)
    extra = jnp.concatenate([nh, nm, nl, one, one, one, zero, zero], axis=0)
    pad = jnp.zeros_like(points)
    return jnp.concatenate([high, high, mid, mid, high, low, extra, pad], axis=0)


def col_side(points):
    high, mid, low = (-2.0 * part for part in split3(points))
    nh, nm, nl = norms3(points)
    one, zero = jnp.ones_like(nh), jnp.zeros_like(nh)
    extra = jnp.concatenate([one, one, one, nh, nm, nl, zero, zero], axis=0)
    pad = jnp.zeros_like(points)
    return jnp.concatenate([high, mid, high, mid, low, high, extra, pad], axis=0)


def matern(dist_sq):
    floor = jnp.maximum(dist_sq, TINY)
    dist = floor * lax.rsqrt(floor)
    decay = jnp.exp2(dist * RATE)
    shifted = dist + HALF3
    return (shifted * shifted + 0.25) * decay


def halves(value):
    high = value.astype(BF16)
    return high, (value - high.astype(F32)).astype(BF16)


def fold(both):
    return both[:PROBES] + both[PROBES:]


def times(vecs, high, low, dims):
    first = lax.dot_general(vecs, high, dims, preferred_element_type=F32)
    return fold(first) + lax.dot_general(vecs[:PROBES], low, dims, preferred_element_type=F32)


OVER_ROWS = (((1,), (0,)), ((), ()))
OVER_COLS = (((1,), (1,)), ((), ()))


def kernel(nb, nc, ls_hbm, feat_hbm, vec_hbm, out_ref, lengthscales, rowbuf, colbuf, rows_t, row_vecs, cols,
           col_vecs, row_acc, col_acc, row_parts, col_parts, dist0, dist1, high0, high1, low0, low1,
           in_sem, row_send, row_recv, relay_send, relay_recv, col_send, col_recv, rp_send, rp_recv, cp_send, cp_recv):
    half = nb // 2
    pairs, chunks, ring = half // 2, nc // 2, nc // 2
    dist, highs, lows = (dist0, dist1), (high0, high1), (low0, low1)
    blk, col = lax.axis_index("blk"), lax.axis_index("col")
    core = blk % 2
    group, chip = blk - core + col % 2, col // 2

    def device(group, chip, core):
        return (group - group % 2 + core, 2 * chip + group % 2)

    own = colbuf.at[half]
    loads = [
        pltpu.make_async_copy(ls_hbm, lengthscales, in_sem.at[0]),
        pltpu.make_async_copy(feat_hbm, own.at[:FEAT], in_sem.at[1]),
        pltpu.make_async_copy(vec_hbm, own.at[FEAT:], in_sem.at[2]),
    ]
    for load in loads:
        load.start()

    def loop(first, last, action):
        def body(step, carry):
            action(step)
            return carry
        lax.fori_loop(first, last, body, 0)

    def row_offset(step):
        return (step + 1) // 2 if step % 2 else ring - step // 2

    def row_peer(step):
        return device(group, (chip + row_offset(step)) % ring, core)

    def row_owner(step, other):
        return device(group, (chip + ring - row_offset(step)) % ring, 1 - core if other else core)

    def col_offset(place):
        return jnp.where(place % 2 == 0, place + 1, nb - 1 - place)

    def col_peer(place):
        return device((group + col_offset(place)) % nb, chip, core)

    def col_owner(place):
        return device((group + nb - col_offset(place)) % nb, chip, core)

    sibling = device(group, chip, 1 - core)
    barrier = pltpu.get_barrier_semaphore()

    def greet(peer):
        pl.semaphore_signal(barrier, inc=1, device_id=peer, device_id_type=MESH)

    greet(sibling)
    for step in range(1, ring):
        greet(row_owner(step, False))
    loop(0, half, lambda place: greet(col_owner(place)))

    row_acc[...] = jnp.zeros_like(row_acc)
    col_acc[...] = jnp.zeros_like(col_acc)
    cols[DEPTH:, :] = jnp.zeros((WIDTH - DEPTH, cols.shape[1]), BF16)
    for load in loads:
        load.wait()
    feature = lax.broadcasted_iota(jnp.int32, (FEAT, WIDTH), 0)
    lengths = jnp.full((FEAT, WIDTH), lengthscales[0], F32)
    for k in range(1, FEAT):
        lengths = jnp.where(feature == k, lengthscales[k], lengths)
    own[:FEAT] = own[:FEAT] / lengths * SCALE
    rowbuf[0, 0] = own[...]
    high1[...] = jnp.zeros_like(high1)
    low1[...] = jnp.zeros_like(low1)
    pl.semaphore_wait(barrier, ring + half)

    def push(source, target, send, recv, device):
        return pltpu.make_async_remote_copy(
            src_ref=source, dst_ref=target, send_sem=send, recv_sem=recv, device_id=device, device_id_type=MESH)

    def row_copy(step):
        return push(own, rowbuf.at[0, step], row_send, row_recv.at[step], row_peer(step))

    def row_relay(step):
        source = rowbuf.at[0, step] if step else own
        return push(source, rowbuf.at[1, step], relay_send, relay_recv.at[step // (ring // 2)], sibling)

    def col_copy(place):
        return push(own, colbuf.at[place], col_send, col_recv.at[place // 2], col_peer(place))

    def row_part(slot):
        return push(row_acc.at[slot], row_parts.at[slot - 1], rp_send, rp_recv, row_owner(slot // 2, slot % 2))

    def col_part(place):
        return push(col_acc.at[place], col_parts.at[place], cp_send, cp_recv, col_owner(place))

    def await_all(region, sem):
        pltpu.make_async_copy(region, region, sem).wait()

    row_relay(0).start()
    for step in range(1, ring // 2):
        row_copy(step).start()
    loop(0, half // 2, lambda place: col_copy(place).start())
    for step in range(ring // 2, ring):
        row_copy(step).start()
    loop(half // 2, half, lambda place: col_copy(place).start())

    def span(place, count):
        return pl.ds(pl.multiple_of(place * WIDTH, WIDTH), count * WIDTH)

    def put_col(place):
        block = colbuf[place]
        at = span(place, 1)
        cols[:DEPTH, at] = col_side(block[:FEAT]).astype(BF16)
        high, low = halves(block[FEAT:])
        col_vecs[:PROBES, at] = high
        col_vecs[PROBES:, at] = low

    def get_pair(pair):
        await_all(colbuf.at[pl.ds(2 * pair, 2)], col_recv.at[pair])
        put_col(2 * pair)
        put_col(2 * pair + 1)

    def pass_rows(side):
        for step in range(side * ring // 2, (side + 1) * ring // 2):
            if step:
                await_all(rowbuf.at[0, step], row_recv.at[step])
                row_relay(step).start()

    def get_rows(side):
        first = side * ring // 2
        await_all(rowbuf.at[1, first:first + ring // 2], relay_recv.at[side])
        for slot in range(2 * first, 2 * first + ring):
            at = slice(slot * WIDTH, (slot + 1) * WIDTH)
            block = rowbuf.at[slot % 2, slot // 2]
            tall = jnp.concatenate([row_side(block[:FEAT]), jnp.zeros((WIDTH - DEPTH, WIDTH), F32)], axis=0)
            rows_t[at, :] = tall.T.astype(BF16)
            high, low = halves(block[FEAT:])
            row_vecs[:PROBES, at] = high
            row_vecs[PROBES:, at] = low

    def inner(slot, place, count, even):
        dist[even][:, :count * WIDTH] = jnp.dot(
            rows_t[span(slot, 2), :], cols[:, span(place, count)], preferred_element_type=F32)

    def elementwise(count, even):
        at = slice(0, count * WIDTH)
        high, low = halves(matern(dist[even][:, at]))
        highs[even][:, at] = high
        lows[even][:, at] = low

    def add_rows(slot, place, even):
        total = times(col_vecs[:, span(place, 2)], highs[even][...], lows[even][...], OVER_COLS)
        for k in range(2):
            row_acc[slot + k] += total[:, k * WIDTH:(k + 1) * WIDTH]

    def add_cols(slot, place, count, even):
        at = slice(0, count * WIDTH)
        total = times(row_vecs[:, span(slot, 2)], highs[even][:, at], lows[even][:, at], OVER_ROWS)
        for k in range(count):
            col_acc[place + k] += total[:, k * WIDTH:(k + 1) * WIDTH]

    quarter, tiles = pairs // 2, nc // 4

    def unit_rows(unit):
        return jnp.where((unit >= quarter) & (unit < 3 * quarter), nc // 2, 0)

    def unit_place(unit):
        return 2 * jnp.where(unit < quarter, unit, jnp.where(unit < 3 * quarter, unit - quarter, unit - 2 * quarter))

    put_col(half)
    pass_rows(0)
    get_rows(0)
    get_pair(0)
    inner(0, 0, 2, 0)

    def one_unit(unit):
        @pl.when((unit < quarter - 1) | ((unit >= 2 * quarter - 1) & (unit < 3 * quarter - 1)))
        def _():
            get_pair(unit_place(unit + 1) // 2)

        @pl.when(unit == quarter // 4)
        def _():
            pass_rows(1)

        @pl.when(unit == quarter - 1)
        def _():
            get_rows(1)

        slots, place = unit_rows(unit), unit_place(unit)
        next_slots = unit_rows(unit + 1)
        next_place = jnp.where(unit == 4 * quarter - 1, half - 2, unit_place(unit + 1))
        old = jnp.maximum(unit - 1, 0)
        old_slots, old_place = unit_rows(old), unit_place(old)
        for tile in range(tiles):
            even, odd = tile % 2, (tile + 1) % 2
            if tile + 1 < tiles:
                inner(slots + 2 * tile + 2, place, 2, odd)
            else:
                inner(next_slots, next_place, 2, odd)
            elementwise(2, even)
            if tile > 0:
                add_cols(slots + 2 * tile - 2, place, 2, odd)
                add_rows(slots + 2 * tile - 2, place, odd)
            else:
                add_cols(old_slots + 2 * tiles - 2, old_place, 2, odd)
                add_rows(old_slots + 2 * tiles - 2, old_place, odd)

        @pl.when(((unit > quarter) & (unit <= 2 * quarter)) | (unit > 3 * quarter))
        def _():
            col_part(old_place).start()
            col_part(old_place + 1).start()

        @pl.when(unit == 3 * quarter)
        def _():
            for slot in range(nc // 2, nc):
                row_part(slot).start()

    loop(0, 4 * quarter, one_unit)
    inner(0, half, 1, 0)
    for chunk in range(chunks + 1):
        even, odd = chunk % 2, (chunk + 1) % 2
        if chunk == 0:
            add_cols(nc // 2 - 2, half - 2, 2, odd)
            add_rows(nc // 2 - 2, half - 2, odd)
            col_part(half - 2).start()
            for slot in range(1, nc // 2):
                row_part(slot).start()
        if chunk + 1 < chunks:
            inner(2 * chunk + 2, half, 1, odd)
        if chunk < chunks:
            elementwise(1, even)
        if chunk > 0:
            add_cols(2 * chunk - 2, half, 1, odd)

    total = row_acc[0] + col_acc[half]
    await_all(col_parts, cp_recv)
    for place in range(half - 1):
        total += col_parts[place]
    await_all(row_parts, rp_recv)
    for slot in range(nc - 1):
        total += row_parts[slot]
    out_ref[...] = total
    await_all(rowbuf.at[0, 1:], row_send)
    await_all(rowbuf.at[1], relay_send)
    await_all(colbuf.at[:half], col_send)
    await_all(row_parts, rp_send)
    await_all(col_parts, cp_send)


def on_device(nb, nc, features, vectors, lengthscales, noise_var, signal):
    half = nb // 2
    sums = pl.pallas_call(
        functools.partial(kernel, nb, nc),
        out_shape=jax.ShapeDtypeStruct((PROBES, WIDTH), F32),
        in_specs=[pl.BlockSpec(memory_space=pltpu.MemorySpace.HBM)] * 3,
        out_specs=pl.BlockSpec(memory_space=pltpu.VMEM),
        scratch_shapes=[
            pltpu.SMEM((FEAT,), F32),
            pltpu.VMEM((2, nc // 2, FEAT + PROBES, WIDTH), F32),
            pltpu.VMEM((half + 1, FEAT + PROBES, WIDTH), F32),
            pltpu.VMEM((nc * WIDTH, WIDTH), BF16),
            pltpu.VMEM((2 * PROBES, nc * WIDTH), BF16),
            pltpu.VMEM((WIDTH, (half + 1) * WIDTH), BF16),
            pltpu.VMEM((2 * PROBES, (half + 1) * WIDTH), BF16),
            pltpu.VMEM((nc, PROBES, WIDTH), F32),
            pltpu.VMEM((half + 1, PROBES, WIDTH), F32),
            pltpu.VMEM((nc - 1, PROBES, WIDTH), F32),
            pltpu.VMEM((half - 1, PROBES, WIDTH), F32),
        ]
        + [pltpu.VMEM((2 * WIDTH, 2 * WIDTH), F32)] * 2
        + [pltpu.VMEM((2 * WIDTH, 2 * WIDTH), BF16)] * 4
        + [
            pltpu.SemaphoreType.DMA((3,)),
            pltpu.SemaphoreType.DMA,
            pltpu.SemaphoreType.DMA((nc // 2,)),
            pltpu.SemaphoreType.DMA,
            pltpu.SemaphoreType.DMA((2,)),
            pltpu.SemaphoreType.DMA,
            pltpu.SemaphoreType.DMA((half // 2,)),
        ]
        + [pltpu.SemaphoreType.DMA] * 4,
        compiler_params=pltpu.CompilerParams(
            collective_id=0, has_side_effects=True, vmem_limit_bytes=60 * 1024 * 1024
        ),
        name="matern_sums",
    )(lengthscales, features, vectors)
    return signal[0] * sums + noise_var[None, :] * vectors


def solution(mesh):
    nb, nc = mesh.shape["blk"], mesh.shape["col"]
    placed = (P(None, ("blk", "col")), P(None, ("blk", "col")), P(), P(("blk", "col")), P())
    return jax.shard_map(
        functools.partial(on_device, nb, nc),
        mesh=mesh,
        in_specs=placed,
        out_specs=P(None, ("blk", "col")),
        check_vma=False,
    )
```

```python
import functools
import math

import jax
import jax.numpy as jnp
from jax import lax
from jax.experimental import pallas as pl
from jax.experimental.pallas import tpu as pltpu
from jax.sharding import PartitionSpec as P

MESH = pl.DeviceIdType.MESH
F32 = jnp.float32
BF16 = jnp.bfloat16
SCALE = math.sqrt(5.0 / 3.0)
HALF3 = math.sqrt(3.0) / 2.0
RATE = -math.sqrt(3.0) * math.log2(math.e)
TINY = 1e-30
WIDTH = 128
FEAT = 8
PROBES = 16
ORDER = (1, 8, 7, 9, 3, 15, 5, 4, 12, 13, 11, 14, 6, 10, 2, 16)
DEPTH = 64


def split3(value):
    high = value.astype(BF16).astype(F32)
    rest = value - high
    mid = rest.astype(BF16).astype(F32)
    return high, mid, rest - mid


def norms3(points):
    return split3(jnp.sum(points * points, axis=0, keepdims=True))


def row_side(points):
    high, mid, low = split3(points)
    nh, nm, nl = norms3(points)
    one, zero = jnp.ones_like(nh), jnp.zeros_like(nh)
    extra = jnp.concatenate([nh, nm, nl, one, one, one, zero, zero], axis=0)
    pad = jnp.zeros_like(points)
    return jnp.concatenate([high, high, mid, mid, high, low, extra, pad], axis=0)


def col_side(points):
    high, mid, low = (-2.0 * part for part in split3(points))
    nh, nm, nl = norms3(points)
    one, zero = jnp.ones_like(nh), jnp.zeros_like(nh)
    extra = jnp.concatenate([one, one, one, nh, nm, nl, zero, zero], axis=0)
    pad = jnp.zeros_like(points)
    return jnp.concatenate([high, mid, high, mid, low, high, extra, pad], axis=0)


def matern(dist_sq):
    floor = jnp.maximum(dist_sq, TINY)
    dist = floor * lax.rsqrt(floor)
    decay = jnp.exp2(dist * RATE)
    shifted = dist + HALF3
    return (shifted * shifted + 0.25) * decay


def halves(value):
    high = value.astype(BF16)
    return high, (value - high.astype(F32)).astype(BF16)


def fold(both):
    return both[:PROBES] + both[PROBES:]


def times(vecs, high, low):
    first = jnp.dot(vecs, high, preferred_element_type=F32)
    return fold(first) + jnp.dot(vecs[:PROBES], low, preferred_element_type=F32)


def kernel(nb, nc, ls_hbm, feat_hbm, vec_hbm, noise_hbm, signal_hbm, out_ref, lengthscales, noise, signal, rowbuf, colbuf, rows_t, row_vecs, cols,
           col_vecs, row_acc, col_acc, row_parts, col_parts, dist0, dist1, high0, high1, low0, low1,
           high_t0, high_t1, low_t0, low_t1, tall0, tall1,
           in_sem, row_send, row_recv, relay_send, relay_recv, col_send, col_recv, rp_send, rp_recv, cp_send, cp_recv):
    half = nb // 2
    pairs, chunks, ring = half // 2, nc // 2, nc // 2
    dist, highs, lows = (dist0, dist1), (high0, high1), (low0, low1)
    highs_t, lows_t = (high_t0, high_t1), (low_t0, low_t1)
    tall = (tall0, tall1)
    blk, col = lax.axis_index("blk"), lax.axis_index("col")
    core = blk % 2
    group, chip = blk - core + col % 2, col // 2

    def device(group, chip, core):
        return (group - group % 2 + core, 2 * chip + group % 2)

    own = colbuf.at[half]
    loads = [
        pltpu.make_async_copy(ls_hbm, lengthscales, in_sem.at[0]),
        pltpu.make_async_copy(feat_hbm, own.at[:FEAT], in_sem.at[1]),
        pltpu.make_async_copy(vec_hbm, own.at[FEAT:], in_sem.at[2]),
        pltpu.make_async_copy(noise_hbm, noise, in_sem.at[3]),
        pltpu.make_async_copy(signal_hbm, signal, in_sem.at[4]),
    ]
    for load in loads:
        load.start()

    def loop(first, last, action):
        def body(step, carry):
            action(step)
            return carry
        lax.fori_loop(first, last, body, 0)

    def row_offset(step):
        return (step + 1) // 2 if step % 2 else ring - step // 2

    def row_peer(step, other=False):
        return device(group, (chip + row_offset(step)) % ring, 1 - core if other else core)

    def row_owner(step, other):
        return device(group, (chip + ring - row_offset(step)) % ring, 1 - core if other else core)

    def col_offset(place):
        return nb - ORDER[place] if place % 2 else ORDER[place]

    def col_peer(place):
        return device((group + col_offset(place)) % nb, chip, core)

    def col_owner(place):
        return device((group + nb - col_offset(place)) % nb, chip, core)

    sibling = device(group, chip, 1 - core)
    barrier = pltpu.get_barrier_semaphore()

    def greet(peer):
        pl.semaphore_signal(barrier, inc=1, device_id=peer, device_id_type=MESH)

    for step in range(ring):
        if step:
            greet(row_owner(step, False))
        if step < ring // 2:
            greet(row_owner(step, True))
    for place in range(half):
        greet(col_owner(place))

    row_acc[...] = jnp.zeros_like(row_acc)
    col_acc[...] = jnp.zeros_like(col_acc)
    cols[DEPTH:, :] = jnp.zeros((WIDTH - DEPTH, cols.shape[1]), BF16)
    for load in loads:
        load.wait()
    feature = lax.broadcasted_iota(jnp.int32, (FEAT, WIDTH), 0)
    lengths = jnp.full((FEAT, WIDTH), lengthscales[0], F32)
    for k in range(1, FEAT):
        lengths = jnp.where(feature == k, lengthscales[k], lengths)
    own[:FEAT] = own[:FEAT] / lengths * SCALE
    rowbuf[0, 0] = own[...]
    for buffer in (high1, low1, high_t1, low_t1):
        buffer[...] = jnp.zeros_like(buffer)
    pl.semaphore_wait(barrier, ring - 1 + ring // 2 + half)

    def push(source, target, send, recv, device):
        return pltpu.make_async_remote_copy(
            src_ref=source, dst_ref=target, send_sem=send, recv_sem=recv, device_id=device, device_id_type=MESH)

    def row_copy(step):
        return push(own, rowbuf.at[0, step], row_send, row_recv.at[step], row_peer(step))

    def row_cross(step):
        if step < ring // 2:
            return push(own, rowbuf.at[1, step], relay_send, relay_recv.at[0], row_peer(step, True))
        return push(rowbuf.at[0, step], rowbuf.at[1, step], relay_send, relay_recv.at[1], sibling)

    def col_copy(place):
        return push(own, colbuf.at[place], col_send, col_recv.at[place // 2], col_peer(place))

    def row_part(slot):
        return push(row_acc.at[slot], row_parts.at[slot - 1], rp_send, rp_recv, row_owner(slot // 2, slot % 2))

    def col_part(place):
        return push(col_acc.at[place], col_parts.at[place], cp_send, cp_recv, col_owner(place))

    def await_all(region, sem):
        pltpu.make_async_copy(region, region, sem).wait()

    for step in range(ring // 2):
        if step:
            row_copy(step).start()
        row_cross(step).start()
    for place in range(half // 2):
        col_copy(place).start()
    for step in range(ring // 2, ring):
        row_copy(step).start()
    for place in range(half // 2, half):
        col_copy(place).start()

    def span(place, count):
        return pl.ds(pl.multiple_of(place * WIDTH, WIDTH), count * WIDTH)

    def put_col(place):
        block = colbuf[place]
        at = span(place, 1)
        cols[:DEPTH, at] = col_side(block[:FEAT]).astype(BF16)
        high, low = halves(block[FEAT:])
        col_vecs[:PROBES, at] = high
        col_vecs[PROBES:, at] = low

    def get_pair(pair):
        await_all(colbuf.at[pl.ds(2 * pair, 2)], col_recv.at[pair])
        put_col(2 * pair)
        put_col(2 * pair + 1)

    def pass_rows():
        for step in range(ring // 2, ring):
            await_all(rowbuf.at[0, step], row_recv.at[step])
            row_cross(step).start()

    def get_rows(side):
        first = side * ring // 2
        if side == 0:
            for step in range(1, ring // 2):
                await_all(rowbuf.at[0, step], row_recv.at[step])
        await_all(rowbuf.at[1, first:first + ring // 2], relay_recv.at[side])
        for slot in range(2 * first, 2 * first + ring):
            at = slice(slot * WIDTH, (slot + 1) * WIDTH)
            block = rowbuf.at[slot % 2, slot // 2]
            tall = jnp.concatenate([row_side(block[:FEAT]), jnp.zeros((WIDTH - DEPTH, WIDTH), F32)], axis=0)
            rows_t[at, :] = tall.T.astype(BF16)
            high, low = halves(block[FEAT:])
            row_vecs[:PROBES, at] = high
            row_vecs[PROBES:, at] = low

    def inner(slot, place, even):
        dist[even][...] = jnp.dot(rows_t[span(slot, 2), :], cols[:, span(place, 2)], preferred_element_type=F32)

    def elementwise(even):
        high, low = halves(matern(dist[even][...]))
        highs[even][...] = high
        lows[even][...] = low
        highs_t[even][...] = high.T
        lows_t[even][...] = low.T

    def add_rows(slot, place, even):
        total = times(col_vecs[:, span(place, 2)], highs_t[even][...], lows_t[even][...])
        for k in range(2):
            row_acc[slot + k] += total[:, k * WIDTH:(k + 1) * WIDTH]

    def add_cols(slot, place, even):
        total = times(row_vecs[:, span(slot, 2)], highs[even][...], lows[even][...])
        for k in range(2):
            col_acc[place + k] += total[:, k * WIDTH:(k + 1) * WIDTH]

    quarter, tiles = pairs // 2, nc // 4

    def unit_rows(unit):
        return jnp.where((unit >= quarter) & (unit < 3 * quarter), nc // 2, 0)

    def unit_place(unit):
        return 2 * jnp.where(unit < quarter, unit, jnp.where(unit < 3 * quarter, unit - quarter, unit - 2 * quarter))

    put_col(half)
    get_rows(0)
    get_pair(0)
    inner(0, 0, 0)

    def units(first, count):
        for step in range(count):
            unit = first + step
            slots, place = unit_rows(unit), unit_place(unit)
            next_slots, next_place = unit_rows(unit + 1), unit_place(jnp.minimum(unit + 1, 4 * quarter - 1))
            old = jnp.maximum(unit - 1, 0)
            old_slots, old_place = unit_rows(old), unit_place(old)
            for tile in range(tiles):
                even, odd = tile % 2, (tile + 1) % 2
                if tile + 1 < tiles:
                    inner(slots + 2 * tile + 2, place, odd)
                else:
                    inner(next_slots, next_place, odd)
                elementwise(even)
                if tile > 0:
                    add_cols(slots + 2 * tile - 2, place, odd)
                    add_rows(slots + 2 * tile - 2, place, odd)
                else:
                    add_cols(old_slots + 2 * tiles - 2, old_place, odd)
                    add_rows(old_slots + 2 * tiles - 2, old_place, odd)

    def send_cols(*ready):
        for pair in ready:
            col_part(2 * pair).start()
            col_part(2 * pair + 1).start()

    def early(unit):
        @pl.when(unit < quarter - 1)
        def _():
            get_pair(unit + 1)

        @pl.when(unit == 1)
        def _():
            pass_rows()

        @pl.when(unit == quarter - 1)
        def _():
            get_rows(1)
        units(unit, 1)

    def late(step):
        first = quarter + 2 * step

        @pl.when(first == 6)
        def _():
            get_pair(4)
            get_pair(5)

        @pl.when(first == 8)
        def _():
            get_pair(6)
            get_pair(7)
        units(first, 2)

        for when, ready in ((4, (0,)), (6, (1, 2)), (8, (3,)), (12, (4,)), (14, (5, 6))):
            @pl.when(first == when)
            def _():
                send_cols(*ready)
                if when == 12:
                    for slot in range(nc // 2, nc):
                        row_part(slot).start()

    loop(0, quarter, early)
    loop(0, 3 * quarter // 2, late)
    def own_inner(tile):
        tall[tile % 2][...] = jnp.dot(
            rows_t[span(4 * tile, 4), :], cols[:, span(half, 1)], preferred_element_type=F32)

    own_inner(0)
    add_cols(nc // 2 - 2, half - 2, 1)
    add_rows(nc // 2 - 2, half - 2, 1)
    col_part(half - 2).start()
    for slot in range(1, nc // 2):
        row_part(slot).start()
    total = row_acc[0]
    for tile in range(tiles):
        if tile + 1 < tiles:
            own_inner(tile + 1)
        high, low = halves(matern(tall[tile % 2][...]))
        total += times(row_vecs[:, span(4 * tile, 4)], high, low)

    await_all(col_parts, cp_recv)
    for place in range(half - 1):
        total += col_parts[place]
    await_all(row_parts, rp_recv)
    for slot in range(nc - 1):
        total += row_parts[slot]
    out_ref[...] = signal[0] * total + noise[...] * own[FEAT:]
    await_all(rowbuf.at[0, 1:], row_send)
    await_all(rowbuf.at[1], relay_send)
    await_all(colbuf.at[:half], col_send)
    await_all(row_parts, rp_send)
    await_all(col_parts, cp_send)


def on_device(nb, nc, features, vectors, lengthscales, noise_var, signal):
    half = nb // 2
    return pl.pallas_call(
        functools.partial(kernel, nb, nc),
        out_shape=jax.ShapeDtypeStruct((PROBES, WIDTH), F32),
        in_specs=[pl.BlockSpec(memory_space=pltpu.MemorySpace.HBM)] * 5,
        out_specs=pl.BlockSpec(memory_space=pltpu.VMEM),
        scratch_shapes=[
            pltpu.SMEM((FEAT,), F32),
            pltpu.VMEM((1, WIDTH), F32),
            pltpu.SMEM((1,), F32),
            pltpu.VMEM((2, nc // 2, FEAT + PROBES, WIDTH), F32),
            pltpu.VMEM((half + 1, FEAT + PROBES, WIDTH), F32),
            pltpu.VMEM((nc * WIDTH, WIDTH), BF16),
            pltpu.VMEM((2 * PROBES, nc * WIDTH), BF16),
            pltpu.VMEM((WIDTH, (half + 1) * WIDTH), BF16),
            pltpu.VMEM((2 * PROBES, (half + 1) * WIDTH), BF16),
            pltpu.VMEM((nc, PROBES, WIDTH), F32),
            pltpu.VMEM((half, PROBES, WIDTH), F32),
            pltpu.VMEM((nc - 1, PROBES, WIDTH), F32),
            pltpu.VMEM((half - 1, PROBES, WIDTH), F32),
        ]
        + [pltpu.VMEM((2 * WIDTH, 2 * WIDTH), F32)] * 2
        + [pltpu.VMEM((2 * WIDTH, 2 * WIDTH), BF16)] * 8
        + [pltpu.VMEM((4 * WIDTH, WIDTH), F32)] * 2
        + [
            pltpu.SemaphoreType.DMA((5,)),
            pltpu.SemaphoreType.DMA,
            pltpu.SemaphoreType.DMA((nc // 2,)),
            pltpu.SemaphoreType.DMA,
            pltpu.SemaphoreType.DMA((2,)),
            pltpu.SemaphoreType.DMA,
            pltpu.SemaphoreType.DMA((half // 2,)),
        ]
        + [pltpu.SemaphoreType.DMA] * 4,
        compiler_params=pltpu.CompilerParams(
            collective_id=0, has_side_effects=True, vmem_limit_bytes=60 * 1024 * 1024
        ),
        name="matern_sums",
    )(lengthscales, features, vectors, noise_var.reshape(1, WIDTH), signal)


def solution(mesh):
    nb, nc = mesh.shape["blk"], mesh.shape["col"]
    assert (nb, nc) == (2 * len(ORDER), 16)
    placed = (P(None, ("blk", "col")), P(None, ("blk", "col")), P(), P(("blk", "col")), P())
    return jax.shard_map(
        functools.partial(on_device, nb, nc),
        mesh=mesh,
        in_specs=placed,
        out_specs=P(None, ("blk", "col")),
        check_vma=False,
    )
```

```python
import functools
import math

import jax
import jax.numpy as jnp
from jax import lax
from jax.experimental import pallas as pl
from jax.experimental.pallas import tpu as pltpu
from jax.sharding import PartitionSpec as P

MESH = pl.DeviceIdType.MESH
F32 = jnp.float32
BF16 = jnp.bfloat16
SCALE = math.sqrt(5.0 / 3.0)
HALF3 = math.sqrt(3.0) / 2.0
RATE = -math.sqrt(3.0) * math.log2(math.e)
TINY = 1e-30
WIDTH = 128
FEAT = 8
PROBES = 16
ORDER = (1, 8, 7, 9, 3, 15, 5, 4, 12, 13, 11, 14, 6, 10, 2, 16)
DEPTH = 64


def split3(value):
    high = value.astype(BF16).astype(F32)
    rest = value - high
    mid = rest.astype(BF16).astype(F32)
    return high, mid, rest - mid


def norms3(points):
    return split3(jnp.sum(points * points, axis=0, keepdims=True))


def row_side(points):
    high, mid, low = split3(points)
    nh, nm, nl = norms3(points)
    one, zero = jnp.ones_like(nh), jnp.zeros_like(nh)
    extra = jnp.concatenate([nh, nm, nl, one, one, one, zero, zero], axis=0)
    pad = jnp.zeros_like(points)
    return jnp.concatenate([high, high, mid, mid, high, low, extra, pad], axis=0)


def col_side(points):
    high, mid, low = (-2.0 * part for part in split3(points))
    nh, nm, nl = norms3(points)
    one, zero = jnp.ones_like(nh), jnp.zeros_like(nh)
    extra = jnp.concatenate([one, one, one, nh, nm, nl, zero, zero], axis=0)
    pad = jnp.zeros_like(points)
    return jnp.concatenate([high, mid, high, mid, low, high, extra, pad], axis=0)


def matern(dist_sq):
    floor = jnp.maximum(dist_sq, TINY)
    dist = floor * lax.rsqrt(floor)
    decay = jnp.exp2(dist * RATE)
    shifted = dist + HALF3
    return (shifted * shifted + 0.25) * decay


def halves(value):
    high = value.astype(BF16)
    return high, (value - high.astype(F32)).astype(BF16)


def fold(both):
    return both[:PROBES] + both[PROBES:]


def times(vecs, high, low):
    first = jnp.dot(vecs, high, preferred_element_type=F32)
    return fold(first) + jnp.dot(vecs[:PROBES], low, preferred_element_type=F32)


def kernel(nb, nc, ls_hbm, feat_hbm, vec_hbm, noise_hbm, signal_hbm, out_ref, lengthscales, noise, signal, rowbuf, colbuf, rows_t, row_vecs, cols,
           col_vecs, row_acc, col_acc, row_parts, col_parts, dist0, dist1, high0, high1, low0, low1,
           high_t0, high_t1, low_t0, low_t1, tall0, tall1,
           in_sem, row_send, row_recv, relay_send, relay_recv, col_send, col_recv, rp_send, rp_recv, cp_send, cp_recv):
    half = nb // 2
    pairs, chunks, ring = half // 2, nc // 2, nc // 2
    dist, highs, lows = (dist0, dist1), (high0, high1), (low0, low1)
    highs_t, lows_t = (high_t0, high_t1), (low_t0, low_t1)
    tall = (tall0, tall1)
    blk, col = lax.axis_index("blk"), lax.axis_index("col")
    core = blk % 2
    group, chip = blk - core + col % 2, col // 2

    def device(group, chip, core):
        return (group - group % 2 + core, 2 * chip + group % 2)

    own = colbuf.at[half]
    loads = [
        pltpu.make_async_copy(ls_hbm, lengthscales, in_sem.at[0]),
        pltpu.make_async_copy(feat_hbm, own.at[:FEAT], in_sem.at[1]),
        pltpu.make_async_copy(vec_hbm, own.at[FEAT:], in_sem.at[2]),
        pltpu.make_async_copy(noise_hbm, noise, in_sem.at[3]),
        pltpu.make_async_copy(signal_hbm, signal, in_sem.at[4]),
    ]
    for load in loads:
        load.start()

    def loop(first, last, action):
        def body(step, carry):
            action(step)
            return carry
        lax.fori_loop(first, last, body, 0)

    def row_offset(step):
        if isinstance(step, int):
            return (step + 1) // 2 if step % 2 else ring - step // 2
        return jnp.where(step % 2 == 1, (step + 1) // 2, ring - step // 2)

    def row_peer(step, other=False):
        return device(group, (chip + row_offset(step)) % ring, 1 - core if other else core)

    def row_owner(step, other):
        return device(group, (chip + ring - row_offset(step)) % ring, (core + other) % 2)

    offsets = [nb - far if place % 2 else far for place, far in enumerate(ORDER)]

    def col_offset(place):
        if isinstance(place, int):
            return offsets[place]
        offset = offsets[0]
        for k in range(1, half):
            offset = jnp.where(place == k, offsets[k], offset)
        return offset

    def col_peer(place):
        return device((group + col_offset(place)) % nb, chip, core)

    def col_owner(place):
        return device((group + nb - col_offset(place)) % nb, chip, core)

    sibling = device(group, chip, 1 - core)
    barrier = pltpu.get_barrier_semaphore()

    def greet(peer):
        pl.semaphore_signal(barrier, inc=1, device_id=peer, device_id_type=MESH)

    for step in range(ring):
        if step:
            greet(row_owner(step, 0))
        if step < ring // 2:
            greet(row_owner(step, 1))
    for place in range(half):
        greet(col_owner(place))

    row_acc[...] = jnp.zeros_like(row_acc)
    col_acc[...] = jnp.zeros_like(col_acc)
    cols[DEPTH:, :] = jnp.zeros((WIDTH - DEPTH, cols.shape[1]), BF16)
    for load in loads:
        load.wait()
    feature = lax.broadcasted_iota(jnp.int32, (FEAT, WIDTH), 0)
    lengths = jnp.full((FEAT, WIDTH), lengthscales[0], F32)
    for k in range(1, FEAT):
        lengths = jnp.where(feature == k, lengthscales[k], lengths)
    own[:FEAT] = own[:FEAT] / lengths * SCALE
    rowbuf[0, 0] = own[...]
    for buffer in (high1, low1, high_t1, low_t1):
        buffer[...] = jnp.zeros_like(buffer)
    pl.semaphore_wait(barrier, ring - 1 + ring // 2 + half)

    def push(source, target, send, recv, device):
        return pltpu.make_async_remote_copy(
            src_ref=source, dst_ref=target, send_sem=send, recv_sem=recv, device_id=device, device_id_type=MESH)

    def row_copy(step):
        return push(own, rowbuf.at[0, step], row_send, row_recv.at[step], row_peer(step))

    def row_cross(step):
        if step < ring // 2:
            return push(own, rowbuf.at[1, step], relay_send, relay_recv.at[0], row_peer(step, True))
        return push(rowbuf.at[0, step], rowbuf.at[1, step], relay_send, relay_recv.at[1], sibling)

    def col_copy(place):
        return push(own, colbuf.at[place], col_send, col_recv.at[place // 2], col_peer(place))

    def row_part(slot):
        return push(row_acc.at[slot], row_parts.at[slot - 1], rp_send, rp_recv, row_owner(slot // 2, slot % 2))

    def col_part(place):
        return push(col_acc.at[place], col_parts.at[place], cp_send, cp_recv, col_owner(place))

    def await_all(region, sem):
        pltpu.make_async_copy(region, region, sem).wait()

    for step in range(ring // 2):
        if step:
            row_copy(step).start()
        row_cross(step).start()
    for place in range(half // 2):
        col_copy(place).start()
    for step in range(ring // 2, ring):
        row_copy(step).start()
    for place in range(half // 2, half):
        col_copy(place).start()

    def span(place, count):
        return pl.ds(pl.multiple_of(place * WIDTH, WIDTH), count * WIDTH)

    def put_col(place):
        block = colbuf[place]
        at = span(place, 1)
        cols[:DEPTH, at] = col_side(block[:FEAT]).astype(BF16)
        high, low = halves(block[FEAT:])
        col_vecs[:PROBES, at] = high
        col_vecs[PROBES:, at] = low

    def get_pair(pair):
        await_all(colbuf.at[pl.ds(2 * pair, 2)], col_recv.at[pair])
        put_col(2 * pair)
        put_col(2 * pair + 1)

    def pass_rows():
        for step in range(ring // 2, ring):
            await_all(rowbuf.at[0, step], row_recv.at[step])
            row_cross(step).start()

    def get_rows(side):
        first = side * ring // 2
        if side == 0:
            for step in range(1, ring // 2):
                await_all(rowbuf.at[0, step], row_recv.at[step])
        await_all(rowbuf.at[1, first:first + ring // 2], relay_recv.at[side])
        for slot in range(2 * first, 2 * first + ring):
            at = slice(slot * WIDTH, (slot + 1) * WIDTH)
            block = rowbuf.at[slot % 2, slot // 2]
            tall = jnp.concatenate([row_side(block[:FEAT]), jnp.zeros((WIDTH - DEPTH, WIDTH), F32)], axis=0)
            rows_t[at, :] = tall.T.astype(BF16)
            high, low = halves(block[FEAT:])
            row_vecs[:PROBES, at] = high
            row_vecs[PROBES:, at] = low

    def inner(slot, place, even):
        dist[even][...] = jnp.dot(rows_t[span(slot, 2), :], cols[:, span(place, 2)], preferred_element_type=F32)

    def elementwise(even):
        high, low = halves(matern(dist[even][...]))
        highs[even][...] = high
        lows[even][...] = low
        highs_t[even][...] = high.T
        lows_t[even][...] = low.T

    def add_rows(slot, place, even):
        total = times(col_vecs[:, span(place, 2)], highs_t[even][...], lows_t[even][...])
        for k in range(2):
            row_acc[slot + k] += total[:, k * WIDTH:(k + 1) * WIDTH]

    def add_cols(slot, place, even):
        total = times(row_vecs[:, span(slot, 2)], highs[even][...], lows[even][...])
        for k in range(2):
            col_acc[place + k] += total[:, k * WIDTH:(k + 1) * WIDTH]

    quarter, tiles = pairs // 2, nc // 4

    def unit_rows(unit):
        return jnp.where((unit >= quarter) & (unit < 3 * quarter), nc // 2, 0)

    def unit_place(unit):
        return 2 * jnp.where(unit < quarter, unit, jnp.where(unit < 3 * quarter, unit - quarter, unit - 2 * quarter))

    put_col(half)
    get_rows(0)
    get_pair(0)
    inner(0, 0, 0)

    def units(first, count):
        for step in range(count):
            unit = first + step
            slots, place = unit_rows(unit), unit_place(unit)
            next_slots, next_place = unit_rows(unit + 1), unit_place(jnp.minimum(unit + 1, 4 * quarter - 1))
            old = jnp.maximum(unit - 1, 0)
            old_slots, old_place = unit_rows(old), unit_place(old)
            for tile in range(tiles):
                even, odd = tile % 2, (tile + 1) % 2
                if tile + 1 < tiles:
                    inner(slots + 2 * tile + 2, place, odd)
                else:
                    inner(next_slots, next_place, odd)
                elementwise(even)
                if tile > 0:
                    add_cols(slots + 2 * tile - 2, place, odd)
                    add_rows(slots + 2 * tile - 2, place, odd)
                else:
                    add_cols(old_slots + 2 * tiles - 2, old_place, odd)
                    add_rows(old_slots + 2 * tiles - 2, old_place, odd)

    def early(unit):
        @pl.when(unit < quarter - 1)
        def _():
            get_pair(unit + 1)

        @pl.when(unit == 1)
        def _():
            pass_rows()

        @pl.when(unit == quarter - 1)
        def _():
            get_rows(1)
        units(unit, 1)

    def late(step):
        first = quarter + 2 * step

        @pl.when(first == 6)
        def _():
            get_pair(4)
            get_pair(5)

        @pl.when(first == 8)
        def _():
            get_pair(6)
            get_pair(7)
        units(first, 2)

        whole = {2: 0, 4: 1, 6: 3, 8: 4, 10: 4, 12: 5, 14: 7}
        start = stop = 0
        for now in range(4, 16, 2):
            start = jnp.where(first == now, 2 * whole[now - 2], start)
            stop = jnp.where(first == now, 2 * whole[now], stop)
        loop(start, stop, lambda place: col_part(place).start())
        loop(nc // 2, jnp.where(first == 12, nc, nc // 2), lambda slot: row_part(slot).start())

    loop(0, quarter, early)
    loop(0, 3 * quarter // 2, late)
    def own_inner(tile):
        tall[tile % 2][...] = jnp.dot(
            rows_t[span(4 * tile, 4), :], cols[:, span(half, 1)], preferred_element_type=F32)

    own_inner(0)
    add_cols(nc // 2 - 2, half - 2, 1)
    add_rows(nc // 2 - 2, half - 2, 1)
    col_part(half - 2).start()
    for slot in range(1, nc // 2):
        row_part(slot).start()
    total = row_acc[0]
    for tile in range(tiles):
        if tile + 1 < tiles:
            own_inner(tile + 1)
        high, low = halves(matern(tall[tile % 2][...]))
        total += times(row_vecs[:, span(4 * tile, 4)], high, low)

    await_all(col_parts, cp_recv)
    for place in range(half - 1):
        total += col_parts[place]
    await_all(row_parts, rp_recv)
    for slot in range(nc - 1):
        total += row_parts[slot]
    out_ref[...] = signal[0] * total + noise[...] * own[FEAT:]
    await_all(rowbuf.at[0, 1:], row_send)
    await_all(rowbuf.at[1], relay_send)
    await_all(colbuf.at[:half], col_send)
    await_all(row_parts, rp_send)
    await_all(col_parts, cp_send)


def on_device(nb, nc, features, vectors, lengthscales, noise_var, signal):
    half = nb // 2
    return pl.pallas_call(
        functools.partial(kernel, nb, nc),
        out_shape=pltpu.VMEM((PROBES, WIDTH), F32),
        in_specs=[pl.BlockSpec(memory_space=pltpu.MemorySpace.HBM)] * 5,
        out_specs=pl.BlockSpec(memory_space=pltpu.VMEM),
        scratch_shapes=[
            pltpu.SMEM((FEAT,), F32),
            pltpu.VMEM((1, WIDTH), F32),
            pltpu.SMEM((1,), F32),
            pltpu.VMEM((2, nc // 2, FEAT + PROBES, WIDTH), F32),
            pltpu.VMEM((half + 1, FEAT + PROBES, WIDTH), F32),
            pltpu.VMEM((nc * WIDTH, WIDTH), BF16),
            pltpu.VMEM((2 * PROBES, nc * WIDTH), BF16),
            pltpu.VMEM((WIDTH, (half + 1) * WIDTH), BF16),
            pltpu.VMEM((2 * PROBES, (half + 1) * WIDTH), BF16),
            pltpu.VMEM((nc, PROBES, WIDTH), F32),
            pltpu.VMEM((half, PROBES, WIDTH), F32),
            pltpu.VMEM((nc - 1, PROBES, WIDTH), F32),
            pltpu.VMEM((half - 1, PROBES, WIDTH), F32),
        ]
        + [pltpu.VMEM((2 * WIDTH, 2 * WIDTH), F32)] * 2
        + [pltpu.VMEM((2 * WIDTH, 2 * WIDTH), BF16)] * 8
        + [pltpu.VMEM((4 * WIDTH, WIDTH), F32)] * 2
        + [
            pltpu.SemaphoreType.DMA((5,)),
            pltpu.SemaphoreType.DMA,
            pltpu.SemaphoreType.DMA((nc // 2,)),
            pltpu.SemaphoreType.DMA,
            pltpu.SemaphoreType.DMA((2,)),
            pltpu.SemaphoreType.DMA,
            pltpu.SemaphoreType.DMA((half // 2,)),
        ]
        + [pltpu.SemaphoreType.DMA] * 4,
        compiler_params=pltpu.CompilerParams(
            collective_id=0, has_side_effects=True, vmem_limit_bytes=60 * 1024 * 1024
        ),
        name="matern_sums",
    )(lengthscales, features, vectors, noise_var.reshape(1, WIDTH), signal)


def solution(mesh):
    nb, nc = mesh.shape["blk"], mesh.shape["col"]
    assert (nb, nc) == (2 * len(ORDER), 16)
    placed = (P(None, ("blk", "col")), P(None, ("blk", "col")), P(), P(("blk", "col")), P())
    return jax.shard_map(
        functools.partial(on_device, nb, nc),
        mesh=mesh,
        in_specs=placed,
        out_specs=P(None, ("blk", "col")),
        check_vma=False,
    )
```

```python
import functools
import math

import jax
import jax.numpy as jnp
from jax import lax
from jax.experimental import pallas as pl
from jax.experimental.pallas import tpu as pltpu
from jax.sharding import PartitionSpec as P

MESH = pl.DeviceIdType.MESH
F32 = jnp.float32
BF16 = jnp.bfloat16
SCALE = math.sqrt(5.0 / 3.0)
HALF3 = math.sqrt(3.0) / 2.0
RATE = -math.sqrt(3.0) * math.log2(math.e)
TINY = 1e-30
WIDTH = 128
FEAT = 8
PROBES = 16
ORDER = (1, 8, 7, 9, 3, 15, 5, 4, 12, 13, 11, 14, 6, 10, 2, 16)
DEPTH = 64


def split3(value):
    high = value.astype(BF16).astype(F32)
    rest = value - high
    mid = rest.astype(BF16).astype(F32)
    return high, mid, rest - mid


def norms3(points):
    return split3(jnp.sum(points * points, axis=0, keepdims=True))


def row_side(points):
    high, mid, low = split3(points)
    nh, nm, nl = norms3(points)
    one, zero = jnp.ones_like(nh), jnp.zeros_like(nh)
    extra = jnp.concatenate([nh, nm, nl, one, one, one, zero, zero], axis=0)
    pad = jnp.zeros_like(points)
    return jnp.concatenate([high, high, mid, mid, high, low, extra, pad], axis=0)


def col_side(points):
    high, mid, low = (-2.0 * part for part in split3(points))
    nh, nm, nl = norms3(points)
    one, zero = jnp.ones_like(nh), jnp.zeros_like(nh)
    extra = jnp.concatenate([one, one, one, nh, nm, nl, zero, zero], axis=0)
    pad = jnp.zeros_like(points)
    return jnp.concatenate([high, mid, high, mid, low, high, extra, pad], axis=0)


def matern(dist_sq):
    floor = jnp.maximum(dist_sq, TINY)
    dist = floor * lax.rsqrt(floor)
    decay = jnp.exp2(dist * RATE)
    shifted = dist + HALF3
    return (shifted * shifted + 0.25) * decay


def halves(value):
    high = value.astype(BF16)
    return high, (value - high.astype(F32)).astype(BF16)


def fold(both):
    return both[:PROBES] + both[PROBES:]


def times(vecs, high, low):
    first = jnp.dot(vecs, high, preferred_element_type=F32)
    return fold(first) + jnp.dot(vecs[:PROBES], low, preferred_element_type=F32)


def kernel(nb, nc, ls_hbm, feat_hbm, vec_hbm, noise_hbm, signal_hbm, out_ref, lengthscales, noise, signal, rowbuf, colbuf, rows_t, row_vecs, cols,
           col_vecs, row_acc, col_acc, row_parts, col_parts, dist0, dist1, high0, high1, low0, low1,
           high_t0, high_t1, low_t0, low_t1, tall0, tall1,
           in_sem, row_send, row_recv, relay_send, relay_recv, col_send, col_recv, rp_send, rp_recv, cp_send, cp_recv):
    half = nb // 2
    pairs, chunks, ring = half // 2, nc // 2, nc // 2
    dist, highs, lows = (dist0, dist1), (high0, high1), (low0, low1)
    highs_t, lows_t = (high_t0, high_t1), (low_t0, low_t1)
    tall = (tall0, tall1)
    blk, col = lax.axis_index("blk"), lax.axis_index("col")
    core = blk % 2
    group, chip = blk - core + col % 2, col // 2

    def device(group, chip, core):
        return (group - group % 2 + core, 2 * chip + group % 2)

    own = colbuf.at[half]
    loads = [
        pltpu.make_async_copy(ls_hbm, lengthscales, in_sem.at[0]),
        pltpu.make_async_copy(feat_hbm, own.at[:FEAT], in_sem.at[1]),
        pltpu.make_async_copy(vec_hbm, own.at[FEAT:], in_sem.at[2]),
        pltpu.make_async_copy(noise_hbm, noise, in_sem.at[3]),
        pltpu.make_async_copy(signal_hbm, signal, in_sem.at[4]),
    ]
    for load in loads:
        load.start()

    def loop(first, last, action):
        def body(step, carry):
            action(step)
            return carry
        lax.fori_loop(first, last, body, 0)

    def row_offset(step):
        if isinstance(step, int):
            return (step + 1) // 2 if step % 2 else ring - step // 2
        return jnp.where(step % 2 == 1, (step + 1) // 2, ring - step // 2)

    def row_peer(step, other=False):
        return device(group, (chip + row_offset(step)) % ring, 1 - core if other else core)

    def row_owner(step, other):
        return device(group, (chip + ring - row_offset(step)) % ring, (core + other) % 2)

    offsets = [nb - far if place % 2 else far for place, far in enumerate(ORDER)]

    def col_offset(place):
        if isinstance(place, int):
            return offsets[place]
        offset = offsets[0]
        for k in range(1, half):
            offset = jnp.where(place == k, offsets[k], offset)
        return offset

    def col_peer(place):
        return device((group + col_offset(place)) % nb, chip, core)

    def col_owner(place):
        return device((group + nb - col_offset(place)) % nb, chip, core)

    sibling = device(group, chip, 1 - core)
    barrier = pltpu.get_barrier_semaphore()

    def greet(peer):
        pl.semaphore_signal(barrier, inc=1, device_id=peer, device_id_type=MESH)

    for place in reversed(range(half)):
        greet(col_owner(place))
    for step in reversed(range(ring)):
        if step:
            greet(row_owner(step, 0))
        if step < ring // 2:
            greet(row_owner(step, 1))

    row_acc[...] = jnp.zeros_like(row_acc)
    col_acc[...] = jnp.zeros_like(col_acc)
    cols[DEPTH:, :] = jnp.zeros((WIDTH - DEPTH, cols.shape[1]), BF16)
    for load in loads:
        load.wait()
    feature = lax.broadcasted_iota(jnp.int32, (FEAT, WIDTH), 0)
    lengths = jnp.full((FEAT, WIDTH), lengthscales[0], F32)
    for k in range(1, FEAT):
        lengths = jnp.where(feature == k, lengthscales[k], lengths)
    own[:FEAT] = own[:FEAT] / lengths * SCALE
    rowbuf[0, 0] = own[...]
    for buffer in (high1, low1, high_t1, low_t1):
        buffer[...] = jnp.zeros_like(buffer)
    pl.semaphore_wait(barrier, ring - 1 + ring // 2 + half)

    def push(source, target, send, recv, device):
        return pltpu.make_async_remote_copy(
            src_ref=source, dst_ref=target, send_sem=send, recv_sem=recv, device_id=device, device_id_type=MESH)

    def row_copy(step):
        return push(own, rowbuf.at[0, step], row_send, row_recv.at[step], row_peer(step))

    def row_cross(step):
        if step < ring // 2:
            return push(own, rowbuf.at[1, step], relay_send, relay_recv.at[0], row_peer(step, True))
        return push(rowbuf.at[0, step], rowbuf.at[1, step], relay_send, relay_recv.at[1], sibling)

    def col_copy(place):
        return push(own, colbuf.at[place], col_send, col_recv.at[place // 2], col_peer(place))

    def row_part(slot):
        return push(row_acc.at[slot], row_parts.at[slot - 1], rp_send, rp_recv, row_owner(slot // 2, slot % 2))

    def col_part(place):
        return push(col_acc.at[place], col_parts.at[place], cp_send, cp_recv, col_owner(place))

    def await_all(region, sem):
        pltpu.make_async_copy(region, region, sem).wait()

    for step in range(ring // 2):
        if step:
            row_copy(step).start()
        row_cross(step).start()
    for place in range(half // 2):
        col_copy(place).start()
    for step in range(ring // 2, ring):
        row_copy(step).start()
    for place in range(half // 2, half):
        col_copy(place).start()

    def span(place, count):
        return pl.ds(pl.multiple_of(place * WIDTH, WIDTH), count * WIDTH)

    def put_col(place):
        block = colbuf[place]
        at = span(place, 1)
        cols[:DEPTH, at] = col_side(block[:FEAT]).astype(BF16)
        high, low = halves(block[FEAT:])
        col_vecs[:PROBES, at] = high
        col_vecs[PROBES:, at] = low

    def get_pair(pair):
        await_all(colbuf.at[pl.ds(2 * pair, 2)], col_recv.at[pair])
        put_col(2 * pair)
        put_col(2 * pair + 1)

    def pass_rows():
        for step in range(ring // 2, ring):
            await_all(rowbuf.at[0, step], row_recv.at[step])
            row_cross(step).start()

    def get_rows(side):
        first = side * ring // 2
        if side == 0:
            for step in range(1, ring // 2):
                await_all(rowbuf.at[0, step], row_recv.at[step])
        await_all(rowbuf.at[1, first:first + ring // 2], relay_recv.at[side])
        for slot in range(2 * first, 2 * first + ring):
            at = slice(slot * WIDTH, (slot + 1) * WIDTH)
            block = rowbuf.at[slot % 2, slot // 2]
            tall = jnp.concatenate([row_side(block[:FEAT]), jnp.zeros((WIDTH - DEPTH, WIDTH), F32)], axis=0)
            rows_t[at, :] = tall.T.astype(BF16)
            high, low = halves(block[FEAT:])
            row_vecs[:PROBES, at] = high
            row_vecs[PROBES:, at] = low

    def inner(slot, place, even):
        dist[even][...] = jnp.dot(rows_t[span(slot, 2), :], cols[:, span(place, 2)], preferred_element_type=F32)

    def elementwise(even):
        high, low = halves(matern(dist[even][...]))
        highs[even][...] = high
        lows[even][...] = low
        highs_t[even][...] = high.T
        lows_t[even][...] = low.T

    def add_rows(slot, place, even):
        total = times(col_vecs[:, span(place, 2)], highs_t[even][...], lows_t[even][...])
        for k in range(2):
            row_acc[slot + k] += total[:, k * WIDTH:(k + 1) * WIDTH]

    def add_cols(slot, place, even):
        total = times(row_vecs[:, span(slot, 2)], highs[even][...], lows[even][...])
        for k in range(2):
            col_acc[place + k] += total[:, k * WIDTH:(k + 1) * WIDTH]

    quarter, tiles = pairs // 2, nc // 4

    def unit_rows(unit):
        return jnp.where((unit >= quarter) & (unit < 3 * quarter), nc // 2, 0)

    def unit_place(unit):
        return 2 * jnp.where(unit < quarter, unit, jnp.where(unit < 3 * quarter, unit - quarter, unit - 2 * quarter))

    put_col(half)
    get_rows(0)
    get_pair(0)
    inner(0, 0, 0)

    def units(first, count):
        for step in range(count):
            unit = first + step
            slots, place = unit_rows(unit), unit_place(unit)
            next_slots, next_place = unit_rows(unit + 1), unit_place(jnp.minimum(unit + 1, 4 * quarter - 1))
            old = jnp.maximum(unit - 1, 0)
            old_slots, old_place = unit_rows(old), unit_place(old)
            for tile in range(tiles):
                even, odd = tile % 2, (tile + 1) % 2
                if tile + 1 < tiles:
                    inner(slots + 2 * tile + 2, place, odd)
                else:
                    inner(next_slots, next_place, odd)
                elementwise(even)
                if tile > 0:
                    add_cols(slots + 2 * tile - 2, place, odd)
                    add_rows(slots + 2 * tile - 2, place, odd)
                else:
                    add_cols(old_slots + 2 * tiles - 2, old_place, odd)
                    add_rows(old_slots + 2 * tiles - 2, old_place, odd)

    def early(unit):
        @pl.when(unit < quarter - 1)
        def _():
            get_pair(unit + 1)

        @pl.when(unit == 1)
        def _():
            pass_rows()

        @pl.when(unit == quarter - 1)
        def _():
            get_rows(1)
        units(unit, 1)

    def late(step):
        first = quarter + 2 * step

        @pl.when(first == 6)
        def _():
            get_pair(4)
            get_pair(5)

        @pl.when(first == 8)
        def _():
            get_pair(6)
            get_pair(7)
        units(first, 2)

        whole = {2: 0, 4: 1, 6: 3, 8: 4, 10: 4, 12: 5, 14: 7}
        start = stop = 0
        for now in range(4, 16, 2):
            start = jnp.where(first == now, 2 * whole[now - 2], start)
            stop = jnp.where(first == now, 2 * whole[now], stop)
        loop(start, stop, lambda place: col_part(place).start())
        loop(nc // 2, jnp.where(first == 12, nc, nc // 2), lambda slot: row_part(slot).start())

    loop(0, quarter, early)
    loop(0, 3 * quarter // 2, late)
    def own_inner(tile):
        tall[tile % 2][...] = jnp.dot(
            rows_t[span(4 * tile, 4), :], cols[:, span(half, 1)], preferred_element_type=F32)

    own_inner(0)
    add_cols(nc // 2 - 2, half - 2, 1)
    add_rows(nc // 2 - 2, half - 2, 1)
    col_part(half - 2).start()
    for slot in range(1, nc // 2):
        row_part(slot).start()
    total = row_acc[0]
    for tile in range(tiles):
        if tile + 1 < tiles:
            own_inner(tile + 1)
        high, low = halves(matern(tall[tile % 2][...]))
        total += times(row_vecs[:, span(4 * tile, 4)], high, low)

    await_all(col_parts, cp_recv)
    for place in range(half - 1):
        total += col_parts[place]
    await_all(row_parts, rp_recv)
    for slot in range(nc - 1):
        total += row_parts[slot]
    out_ref[...] = signal[0] * total + noise[...] * own[FEAT:]
    await_all(rowbuf.at[0, 1:], row_send)
    await_all(rowbuf.at[1], relay_send)
    await_all(colbuf.at[:half], col_send)
    await_all(row_parts, rp_send)
    await_all(col_parts, cp_send)


def on_device(nb, nc, features, vectors, lengthscales, noise_var, signal):
    half = nb // 2
    return pl.pallas_call(
        functools.partial(kernel, nb, nc),
        out_shape=pltpu.VMEM((PROBES, WIDTH), F32),
        in_specs=[pl.BlockSpec(memory_space=pltpu.MemorySpace.HBM)] * 5,
        out_specs=pl.BlockSpec(memory_space=pltpu.VMEM),
        scratch_shapes=[
            pltpu.SMEM((FEAT,), F32),
            pltpu.VMEM((1, WIDTH), F32),
            pltpu.SMEM((1,), F32),
            pltpu.VMEM((2, nc // 2, FEAT + PROBES, WIDTH), F32),
            pltpu.VMEM((half + 1, FEAT + PROBES, WIDTH), F32),
            pltpu.VMEM((nc * WIDTH, WIDTH), BF16),
            pltpu.VMEM((2 * PROBES, nc * WIDTH), BF16),
            pltpu.VMEM((WIDTH, (half + 1) * WIDTH), BF16),
            pltpu.VMEM((2 * PROBES, (half + 1) * WIDTH), BF16),
            pltpu.VMEM((nc, PROBES, WIDTH), F32),
            pltpu.VMEM((half, PROBES, WIDTH), F32),
            pltpu.VMEM((nc - 1, PROBES, WIDTH), F32),
            pltpu.VMEM((half - 1, PROBES, WIDTH), F32),
        ]
        + [pltpu.VMEM((2 * WIDTH, 2 * WIDTH), F32)] * 2
        + [pltpu.VMEM((2 * WIDTH, 2 * WIDTH), BF16)] * 8
        + [pltpu.VMEM((4 * WIDTH, WIDTH), F32)] * 2
        + [
            pltpu.SemaphoreType.DMA((5,)),
            pltpu.SemaphoreType.DMA,
            pltpu.SemaphoreType.DMA((nc // 2,)),
            pltpu.SemaphoreType.DMA,
            pltpu.SemaphoreType.DMA((2,)),
            pltpu.SemaphoreType.DMA,
            pltpu.SemaphoreType.DMA((half // 2,)),
        ]
        + [pltpu.SemaphoreType.DMA] * 4,
        compiler_params=pltpu.CompilerParams(
            collective_id=0, has_side_effects=True, vmem_limit_bytes=60 * 1024 * 1024
        ),
        name="matern_sums",
    )(lengthscales, features, vectors, noise_var.reshape(1, WIDTH), signal)


def solution(mesh):
    nb, nc = mesh.shape["blk"], mesh.shape["col"]
    assert (nb, nc) == (2 * len(ORDER), 16)
    placed = (P(None, ("blk", "col")), P(None, ("blk", "col")), P(), P(("blk", "col")), P())
    return jax.shard_map(
        functools.partial(on_device, nb, nc),
        mesh=mesh,
        in_specs=placed,
        out_specs=P(None, ("blk", "col")),
        check_vma=False,
    )
```

```python
import functools
import math

import jax
import jax.numpy as jnp
from jax import lax
from jax.experimental import pallas as pl
from jax.experimental.pallas import tpu as pltpu
from jax.sharding import PartitionSpec as P

MESH = pl.DeviceIdType.MESH
F32 = jnp.float32
BF16 = jnp.bfloat16
SCALE = math.sqrt(5.0 / 3.0)
HALF3 = math.sqrt(3.0) / 2.0
RATE = -math.sqrt(3.0) * math.log2(math.e)
TINY = 1e-30
WIDTH = 128
FEAT = 8
PROBES = 16
ORDER = (1, 8, 7, 9, 3, 15, 5, 4, 12, 13, 11, 14, 6, 10, 2, 16)
DEPTH = 64


def split3(value):
    high = value.astype(BF16).astype(F32)
    rest = value - high
    mid = rest.astype(BF16).astype(F32)
    return high, mid, rest - mid


def norms3(points):
    return split3(jnp.sum(points * points, axis=0, keepdims=True))


def row_side(points):
    high, mid, low = split3(points)
    nh, nm, nl = norms3(points)
    one, zero = jnp.ones_like(nh), jnp.zeros_like(nh)
    extra = jnp.concatenate([nh, nm, nl, one, one, one, zero, zero], axis=0)
    pad = jnp.zeros_like(points)
    return jnp.concatenate([high, high, mid, mid, high, low, extra, pad], axis=0)


def col_side(points):
    high, mid, low = (-2.0 * part for part in split3(points))
    nh, nm, nl = norms3(points)
    one, zero = jnp.ones_like(nh), jnp.zeros_like(nh)
    extra = jnp.concatenate([one, one, one, nh, nm, nl, zero, zero], axis=0)
    pad = jnp.zeros_like(points)
    return jnp.concatenate([high, mid, high, mid, low, high, extra, pad], axis=0)


def matern(dist_sq):
    floor = jnp.maximum(dist_sq, TINY)
    dist = floor * lax.rsqrt(floor)
    decay = jnp.exp2(dist * RATE)
    shifted = dist + HALF3
    return (shifted * shifted + 0.25) * decay


def halves(value):
    high = value.astype(BF16)
    return high, (value - high.astype(F32)).astype(BF16)


def fold(both):
    return both[:PROBES] + both[PROBES:]


def times(vecs, high, low):
    first = jnp.dot(vecs, high, preferred_element_type=F32)
    return fold(first) + jnp.dot(vecs[:PROBES], low, preferred_element_type=F32)


def kernel(nb, nc, ls_hbm, feat_hbm, vec_hbm, noise_hbm, signal_hbm, out_ref, lengthscales, noise, signal, rowbuf, colbuf, rows_t, row_vecs, cols,
           col_vecs, row_acc, col_acc, row_parts, col_parts, dist0, dist1, high0, high1, low0, low1,
           high_t0, high_t1, low_t0, low_t1, tall0, tall1,
           in_sem, row_send, row_recv, relay_send, relay_recv, col_send, col_recv, rp_send, rp_recv, cp_send, cp_recv):
    half = nb // 2
    pairs, chunks, ring = half // 2, nc // 2, nc // 2
    dist, highs, lows = (dist0, dist1), (high0, high1), (low0, low1)
    highs_t, lows_t = (high_t0, high_t1), (low_t0, low_t1)
    tall = (tall0, tall1)
    blk, col = lax.axis_index("blk"), lax.axis_index("col")
    core = blk % 2
    group, chip = blk - core + col % 2, col // 2

    def device(group, chip, core):
        return (group - group % 2 + core, 2 * chip + group % 2)

    own = colbuf.at[half]
    loads = [
        pltpu.make_async_copy(ls_hbm, lengthscales, in_sem.at[0]),
        pltpu.make_async_copy(feat_hbm, own.at[:FEAT], in_sem.at[1]),
        pltpu.make_async_copy(vec_hbm, own.at[FEAT:], in_sem.at[2]),
        pltpu.make_async_copy(noise_hbm, noise, in_sem.at[3]),
        pltpu.make_async_copy(signal_hbm, signal, in_sem.at[4]),
    ]
    for load in loads:
        load.start()

    def loop(first, last, action):
        def body(step, carry):
            action(step)
            return carry
        lax.fori_loop(first, last, body, 0)

    def row_offset(step):
        if isinstance(step, int):
            return (step + 1) // 2 if step % 2 else ring - step // 2
        return jnp.where(step % 2 == 1, (step + 1) // 2, ring - step // 2)

    def row_peer(step, other=False):
        return device(group, (chip + row_offset(step)) % ring, 1 - core if other else core)

    def row_owner(step, other):
        return device(group, (chip + ring - row_offset(step)) % ring, (core + other) % 2)

    offsets = [nb - far if place % 2 else far for place, far in enumerate(ORDER)]

    def col_offset(place):
        if isinstance(place, int):
            return offsets[place]
        offset = offsets[0]
        for k in range(1, half):
            offset = jnp.where(place == k, offsets[k], offset)
        return offset

    def col_peer(place):
        return device((group + col_offset(place)) % nb, chip, core)

    def col_owner(place):
        return device((group + nb - col_offset(place)) % nb, chip, core)

    sibling = device(group, chip, 1 - core)
    barrier = pltpu.get_barrier_semaphore()

    def greet(peer):
        pl.semaphore_signal(barrier, inc=1, device_id=peer, device_id_type=MESH)

    for place in reversed(range(half)):
        greet(col_owner(place))
    for step in reversed(range(ring)):
        if step:
            greet(row_owner(step, 0))
        greet(row_owner(step, 1))

    row_acc[...] = jnp.zeros_like(row_acc)
    col_acc[...] = jnp.zeros_like(col_acc)
    cols[DEPTH:, :] = jnp.zeros((WIDTH - DEPTH, cols.shape[1]), BF16)
    for load in loads:
        load.wait()
    feature = lax.broadcasted_iota(jnp.int32, (FEAT, WIDTH), 0)
    lengths = jnp.full((FEAT, WIDTH), lengthscales[0], F32)
    for k in range(1, FEAT):
        lengths = jnp.where(feature == k, lengthscales[k], lengths)
    own[:FEAT] = own[:FEAT] / lengths * SCALE
    rowbuf[0, 0] = own[...]
    for buffer in (high1, low1, high_t1, low_t1):
        buffer[...] = jnp.zeros_like(buffer)
    pl.semaphore_wait(barrier, ring - 1 + ring + half)

    def push(source, target, send, recv, device):
        return pltpu.make_async_remote_copy(
            src_ref=source, dst_ref=target, send_sem=send, recv_sem=recv, device_id=device, device_id_type=MESH)

    def row_copy(step):
        return push(own, rowbuf.at[0, step], row_send, row_recv.at[step], row_peer(step))

    def row_cross(step):
        return push(own, rowbuf.at[1, step], relay_send, relay_recv.at[step // (ring // 2)], row_peer(step, True))

    def col_copy(place):
        return push(own, colbuf.at[place], col_send, col_recv.at[place // 2], col_peer(place))

    def row_part(slot):
        return push(row_acc.at[slot], row_parts.at[slot - 1], rp_send, rp_recv, row_owner(slot // 2, slot % 2))

    def col_part(place):
        return push(col_acc.at[place], col_parts.at[place], cp_send, cp_recv, col_owner(place))

    def await_all(region, sem):
        pltpu.make_async_copy(region, region, sem).wait()

    for step in range(ring // 2):
        if step:
            row_copy(step).start()
        row_cross(step).start()
    for place in range(half // 2):
        col_copy(place).start()
    for step in range(ring // 2, ring):
        row_copy(step).start()
        row_cross(step).start()
    for place in range(half // 2, half):
        col_copy(place).start()

    def span(place, count):
        return pl.ds(pl.multiple_of(place * WIDTH, WIDTH), count * WIDTH)

    def put_col(place):
        block = colbuf[place]
        at = span(place, 1)
        cols[:DEPTH, at] = col_side(block[:FEAT]).astype(BF16)
        high, low = halves(block[FEAT:])
        col_vecs[:PROBES, at] = high
        col_vecs[PROBES:, at] = low

    def get_pair(pair):
        await_all(colbuf.at[pl.ds(2 * pair, 2)], col_recv.at[pair])
        put_col(2 * pair)
        put_col(2 * pair + 1)

    def get_rows(side):
        first = side * ring // 2
        for step in range(max(first, 1), first + ring // 2):
            await_all(rowbuf.at[0, step], row_recv.at[step])
        await_all(rowbuf.at[1, first:first + ring // 2], relay_recv.at[side])
        for slot in range(2 * first, 2 * first + ring):
            at = slice(slot * WIDTH, (slot + 1) * WIDTH)
            block = rowbuf.at[slot % 2, slot // 2]
            tall = jnp.concatenate([row_side(block[:FEAT]), jnp.zeros((WIDTH - DEPTH, WIDTH), F32)], axis=0)
            rows_t[at, :] = tall.T.astype(BF16)
            high, low = halves(block[FEAT:])
            row_vecs[:PROBES, at] = high
            row_vecs[PROBES:, at] = low

    def inner(slot, place, even):
        dist[even][...] = jnp.dot(rows_t[span(slot, 2), :], cols[:, span(place, 2)], preferred_element_type=F32)

    def elementwise(even):
        high, low = halves(matern(dist[even][...]))
        highs[even][...] = high
        lows[even][...] = low
        highs_t[even][...] = high.T
        lows_t[even][...] = low.T

    def add_rows(slot, place, even):
        total = times(col_vecs[:, span(place, 2)], highs_t[even][...], lows_t[even][...])
        for k in range(2):
            row_acc[slot + k] += total[:, k * WIDTH:(k + 1) * WIDTH]

    def add_cols(slot, place, even):
        total = times(row_vecs[:, span(slot, 2)], highs[even][...], lows[even][...])
        for k in range(2):
            col_acc[place + k] += total[:, k * WIDTH:(k + 1) * WIDTH]

    quarter, tiles = pairs // 2, nc // 4

    def unit_rows(unit):
        return jnp.where((unit >= quarter) & (unit < 3 * quarter), nc // 2, 0)

    def unit_place(unit):
        return 2 * jnp.where(unit < quarter, unit, jnp.where(unit < 3 * quarter, unit - quarter, unit - 2 * quarter))

    put_col(half)
    get_rows(0)
    get_pair(0)
    inner(0, 0, 0)

    def units(first, count):
        for step in range(count):
            unit = first + step
            slots, place = unit_rows(unit), unit_place(unit)
            next_slots, next_place = unit_rows(unit + 1), unit_place(jnp.minimum(unit + 1, 4 * quarter - 1))
            old = jnp.maximum(unit - 1, 0)
            old_slots, old_place = unit_rows(old), unit_place(old)
            for tile in range(tiles):
                even, odd = tile % 2, (tile + 1) % 2
                if tile + 1 < tiles:
                    inner(slots + 2 * tile + 2, place, odd)
                else:
                    inner(next_slots, next_place, odd)
                elementwise(even)
                if tile > 0:
                    add_cols(slots + 2 * tile - 2, place, odd)
                    add_rows(slots + 2 * tile - 2, place, odd)
                else:
                    add_cols(old_slots + 2 * tiles - 2, old_place, odd)
                    add_rows(old_slots + 2 * tiles - 2, old_place, odd)

    def early(unit):
        @pl.when(unit < quarter - 1)
        def _():
            get_pair(unit + 1)

        @pl.when(unit == quarter - 1)
        def _():
            get_rows(1)
        units(unit, 1)

    def late(step):
        first = quarter + 2 * step

        @pl.when(first == 6)
        def _():
            get_pair(4)
            get_pair(5)

        @pl.when(first == 8)
        def _():
            get_pair(6)
            get_pair(7)
        units(first, 2)

        whole = {2: 0, 4: 1, 6: 3, 8: 4, 10: 4, 12: 5, 14: 7}
        start = stop = 0
        for now in range(4, 16, 2):
            start = jnp.where(first == now, 2 * whole[now - 2], start)
            stop = jnp.where(first == now, 2 * whole[now], stop)
        loop(start, stop, lambda place: col_part(place).start())
        loop(nc // 2, jnp.where(first == 12, nc, nc // 2), lambda slot: row_part(slot).start())

    loop(0, quarter, early)
    loop(0, 3 * quarter // 2, late)
    def own_inner(tile):
        tall[tile % 2][...] = jnp.dot(
            rows_t[span(4 * tile, 4), :], cols[:, span(half, 1)], preferred_element_type=F32)

    own_inner(0)
    add_cols(nc // 2 - 2, half - 2, 1)
    add_rows(nc // 2 - 2, half - 2, 1)
    col_part(half - 2).start()
    for slot in range(1, nc // 2):
        row_part(slot).start()
    total = row_acc[0]
    for tile in range(tiles):
        if tile + 1 < tiles:
            own_inner(tile + 1)
        high, low = halves(matern(tall[tile % 2][...]))
        total += times(row_vecs[:, span(4 * tile, 4)], high, low)

    await_all(col_parts, cp_recv)
    for place in range(half - 1):
        total += col_parts[place]
    await_all(row_parts, rp_recv)
    for slot in range(nc - 1):
        total += row_parts[slot]
    out_ref[...] = signal[0] * total + noise[...] * own[FEAT:]
    await_all(rowbuf.at[0, 1:], row_send)
    await_all(rowbuf.at[1], relay_send)
    await_all(colbuf.at[:half], col_send)
    await_all(row_parts, rp_send)
    await_all(col_parts, cp_send)


def on_device(nb, nc, features, vectors, lengthscales, noise_var, signal):
    half = nb // 2
    return pl.pallas_call(
        functools.partial(kernel, nb, nc),
        out_shape=pltpu.VMEM((PROBES, WIDTH), F32),
        in_specs=[pl.BlockSpec(memory_space=pltpu.MemorySpace.HBM)] * 5,
        out_specs=pl.BlockSpec(memory_space=pltpu.VMEM),
        scratch_shapes=[
            pltpu.SMEM((FEAT,), F32),
            pltpu.VMEM((1, WIDTH), F32),
            pltpu.SMEM((1,), F32),
            pltpu.VMEM((2, nc // 2, FEAT + PROBES, WIDTH), F32),
            pltpu.VMEM((half + 1, FEAT + PROBES, WIDTH), F32),
            pltpu.VMEM((nc * WIDTH, WIDTH), BF16),
            pltpu.VMEM((2 * PROBES, nc * WIDTH), BF16),
            pltpu.VMEM((WIDTH, (half + 1) * WIDTH), BF16),
            pltpu.VMEM((2 * PROBES, (half + 1) * WIDTH), BF16),
            pltpu.VMEM((nc, PROBES, WIDTH), F32),
            pltpu.VMEM((half, PROBES, WIDTH), F32),
            pltpu.VMEM((nc - 1, PROBES, WIDTH), F32),
            pltpu.VMEM((half - 1, PROBES, WIDTH), F32),
        ]
        + [pltpu.VMEM((2 * WIDTH, 2 * WIDTH), F32)] * 2
        + [pltpu.VMEM((2 * WIDTH, 2 * WIDTH), BF16)] * 8
        + [pltpu.VMEM((4 * WIDTH, WIDTH), F32)] * 2
        + [
            pltpu.SemaphoreType.DMA((5,)),
            pltpu.SemaphoreType.DMA,
            pltpu.SemaphoreType.DMA((nc // 2,)),
            pltpu.SemaphoreType.DMA,
            pltpu.SemaphoreType.DMA((2,)),
            pltpu.SemaphoreType.DMA,
            pltpu.SemaphoreType.DMA((half // 2,)),
        ]
        + [pltpu.SemaphoreType.DMA] * 4,
        compiler_params=pltpu.CompilerParams(
            collective_id=0, has_side_effects=True, vmem_limit_bytes=60 * 1024 * 1024
        ),
        name="matern_sums",
    )(lengthscales, features, vectors, noise_var.reshape(1, WIDTH), signal)


def solution(mesh):
    nb, nc = mesh.shape["blk"], mesh.shape["col"]
    assert (nb, nc) == (2 * len(ORDER), 16)
    placed = (P(None, ("blk", "col")), P(None, ("blk", "col")), P(), P(("blk", "col")), P())
    return jax.shard_map(
        functools.partial(on_device, nb, nc),
        mesh=mesh,
        in_specs=placed,
        out_specs=P(None, ("blk", "col")),
        check_vma=False,
    )
```
